32 devices in a mesh: zslab: 4 (over y, x), xband: 8 (over z, core).
Axes of the slice: x: 2, y: 2, z: 4, core: 2. Of those that a mesh axis runs over, the one named last changes fastest.
Arguments:
- volume: float32 [8, 128, 512], P('xband', 'zslab'), may hold values from 0.2 to 1.8
- measured: float32 [8, 128, 512], P('xband', 'zslab'), may hold values from 1.6 to 14.4
- magnification: float32 [8, 8], P(None, 'xband'), may hold values from 1.25 to 2
- shift_y: int32 [8, 8], P(None, 'xband'), may hold values from -32 to 32
- shift_z: int32 [8, 8], P(None, 'xband'), may hold values from -4 to 4
Outputs:
- residual: float32 [8, 128, 512], P('xband', 'zslab')
- correction: float32 [8, 128, 512], P('xband', 'zslab')
The draws below stay inside these ranges and needn't reach their ends.
All inputs are finite; a program needn't handle non-finite values.
Results may differ from the reference program's by a relative error of at most 0.0003.
Values sent between devices are 32-bit elements; how exact they have to be, the bound alone decides.
No kernel may reach another device: no remote copies, remote signals or barrier semaphores. Data moves between devices by JAX's collectives and lax.ppermute only.
A program may use at most 64 MiB of HBM per device.

```python
import math
import jax
import jax.numpy as jnp
from jax import lax

Y = 512
HALO = 4
SHIFT = 32
X = 8
Z = 128
ANGLES = 8


def plant(drawn, own_key, low, top_value):
    longest = drawn.shape.index(max(drawn.shape))
    spots = []
    for shift in (0, 1):
        where = [jax.random.randint(jax.random.fold_in(own_key, axis), (), 0, length) for axis, length in enumerate(drawn.shape)]
        where[longest] = (where[longest] + shift) % drawn.shape[longest]
        spots.append(tuple(where))
    return drawn.at[spots[0]].set(low).at[spots[1]].set(top_value)


def shard_levels(stream_key, shape, shards, smallest, top_value):
    level, own = 1.0, jax.random.fold_in(stream_key, 6)
    for dim, blocks in shards:
        heights = jnp.exp(jax.random.uniform(jax.random.fold_in(own, dim), (blocks,), jnp.float32, smallest / len(shards), top_value / len(shards)))
        level = level * jnp.repeat(heights, shape[dim] // blocks).reshape([-1 if axis == dim else 1 for axis in range(len(shape))])
    return level


def setup_inputs(seed: int = 0) -> dict:
    arg_keys = jax.random.split(jax.random.key(seed), 6)
    volume = jnp.clip(0.2 + 1.5999999 * jax.random.uniform(arg_keys[0], (X, Z, Y), jnp.float32) ** shard_levels(arg_keys[0], (X, Z, Y), ((0, 8), (1, 4)), -0.2, 0.2), 0.2, 1.8)
    measured = jnp.clip(1.6 + 12.7999996 * jax.random.uniform(arg_keys[1], (ANGLES, Z, Y), jnp.float32) ** shard_levels(arg_keys[1], (ANGLES, Z, Y), ((0, 8), (1, 4)), -0.2, 0.2), 1.6, 14.4)
    magnification = jnp.clip(1.25 + 0.75 * jax.random.uniform(arg_keys[2], (ANGLES, X), jnp.float32) ** shard_levels(arg_keys[2], (ANGLES, X), ((1, 8),), -0.2, 0.2), 1.25, 2.0)
    shift_y = plant(jax.random.randint(arg_keys[3], (ANGLES, X), 0 - SHIFT, SHIFT + 1), jax.random.fold_in(arg_keys[3], 1), 0 - SHIFT, SHIFT).astype(jnp.int32)
    shift_z = plant(jax.random.randint(arg_keys[4], (ANGLES, X), 0 - HALO, HALO + 1), jax.random.fold_in(arg_keys[4], 1), 0 - HALO, HALO).astype(jnp.int32)
    return {"volume": volume, "measured": measured, "magnification": magnification, "shift_y": shift_y, "shift_z": shift_z}


def tap_tables(magnification, shift_y, index):
    columns = jnp.arange(Y, dtype=jnp.float32)
    centre = (Y - 1) / 2.0
    mags = lax.dynamic_index_in_dim(magnification, index, 1, keepdims=False)
    offsets = lax.dynamic_index_in_dim(shift_y, index, 1, keepdims=False).astype(jnp.float32)
    target = (columns[None, :] - centre) / mags[:, None] + centre + offsets[:, None]
    lower = jnp.floor(target)
    frac = target - lower
    return (lower.astype(jnp.int32), frac)

def reference(volume, measured, magnification, shift_y, shift_z):

    def forward_step(total, index):
        lower, frac = tap_tables(magnification, shift_y, index)
        slab = lax.dynamic_index_in_dim(volume, index, 0, keepdims=False)
        left = jnp.take(slab, lower, axis=1).transpose(1, 0, 2)
        right = jnp.take(slab, lower + 1, axis=1).transpose(1, 0, 2)
        image = (1.0 - frac)[:, None, :] * left + frac[:, None, :] * right
        padded = jnp.pad(image, ((0, 0), (HALO, HALO), (0, 0)))
        rowshift = lax.dynamic_index_in_dim(shift_z, index, 1, keepdims=False)
        placed = jax.vmap(lambda plane, offset: lax.dynamic_slice_in_dim(plane, (HALO - offset).astype(jnp.int32), Z, 0))(padded, rowshift)
        return (total + placed, None)
    proj, unused = lax.scan(forward_step, jnp.zeros((ANGLES, Z, Y), jnp.float32), jnp.arange(X, dtype=jnp.int32))
    gain = lax.optimization_barrier(jnp.sum(measured, axis=1)) / lax.optimization_barrier(jnp.sum(proj, axis=1))
    residual = (measured - gain[:, None, :] * proj) / X
    padded_res = jnp.pad(residual, ((0, 0), (HALO, HALO), (0, 0)))

    def backward_step(carry, index):
        lower, frac = tap_tables(magnification, shift_y, index)
        rowshift = lax.dynamic_index_in_dim(shift_z, index, 1, keepdims=False)
        rows = jax.vmap(lambda plane, offset: lax.dynamic_slice_in_dim(plane, (HALO + offset).astype(jnp.int32), Z, 0))(padded_res, rowshift)
        left_vals = ((1.0 - frac)[:, None, :] * rows).transpose(1, 0, 2).reshape(Z, ANGLES * Y)
        right_vals = (frac[:, None, :] * rows).transpose(1, 0, 2).reshape(Z, ANGLES * Y)
        plane = jnp.zeros((Z, Y), jnp.float32)
        plane = plane.at[:, lower.reshape(-1)].add(left_vals)
        plane = plane.at[:, (lower + 1).reshape(-1)].add(right_vals)
        return (carry, plane)
    unused2, planes = lax.scan(backward_step, jnp.zeros((), jnp.float32), jnp.arange(X, dtype=jnp.int32))
    correction = planes / math.sqrt(ANGLES)
    return (residual, correction)
```

```python
import functools
import math

import jax
import jax.numpy as jnp
from jax import lax
from jax.experimental import pallas as pl
from jax.experimental.pallas import tpu as pltpu
from jax.sharding import PartitionSpec as P

HALO = 4
LANES = 128
VMEM_LIMIT = 48 * 1024 * 1024
NT = (((1,), (1,)), ((), ()))


def rows_at(tile, index):
    return jnp.take_along_axis(tile, index, axis=0, mode="promise_in_bounds")


def by_lane(lane, depth, values):
    out = jnp.full(lane.shape, values[0])
    for q in range(1, len(values)):
        out = jnp.where(lane >= q * depth, values[q], out)
    return out


def two_parts(x):
    high = x.astype(jnp.bfloat16)
    return high, (x - high.astype(jnp.float32)).astype(jnp.bfloat16)


def copy_tables(sources, start, table, sem):
    copies = [
        pltpu.make_async_copy(source.at[pl.ds(start, 8)], table.at[k], sem.at[k])
        for k, source in enumerate(sources)
    ]
    for copy in copies:
        copy.start()
    return copies


def forward_kernel(n, depth, width, slabs, *refs):
    half = n // 2
    info, volumes, measured = refs[0], refs[1 : 1 + n], refs[1 + n : 1 + n + half]
    proj, up, down, sums = refs[1 + n + half : 5 + n + half]
    turned, high, low, table, sem = refs[5 + n + half :]
    tiles = width // LANES
    per = LANES // depth
    groups = n // per
    rows = depth + 2 * HALO
    centre = (width - 1) / 2.0
    band, slab = info[0], info[1]
    copies = copy_tables(volumes, tiles * depth, table, sem)
    for g in range(groups):
        for tile in range(tiles):
            part = pl.ds(tile * depth, depth)
            block = jnp.concatenate([volumes[g * per + q][part, :] for q in range(per)], axis=0)
            turned[g, tile * LANES : (tile + 1) * LANES, :] = block.T
    for copy in copies:
        copy.wait()

    lane = lax.broadcasted_iota(jnp.int32, (8, LANES), 1)
    step = lax.broadcasted_iota(jnp.int32, (8, LANES), 0).astype(jnp.float32)
    place = lax.broadcasted_iota(jnp.int32, (rows, LANES), 0)
    wide_lane = lax.broadcasted_iota(jnp.int32, (rows, LANES), 1)
    keep = (place >= HALO) | (slab > 0)
    keep = keep & ((place < HALO + depth) | (slab < slabs - 1))

    def angle(j, carry):
        a = band ^ (2 * j)
        total = jnp.zeros((rows, width), jnp.float32)
        for g in range(groups):
            inverse = [table[g * per + q, 0, a] for q in range(per)]
            offset = [table[g * per + q, 1, a] for q in range(per)]
            shift = [table[g * per + q, 2, a].astype(jnp.int32) for q in range(per)]
            inverse_l = by_lane(lane, depth, inverse)
            offset_l = by_lane(lane, depth, offset)
            fine = step * inverse_l

            def eight(block):
                first = (block * 8).astype(jnp.float32) - centre
                base = [(first * inverse[q] + offset[q]).astype(jnp.int32) for q in range(per)]
                window = turned[g, pl.ds(base[0], 8), :]
                for q in range(1, per):
                    window = jnp.where(lane >= q * depth, turned[g, pl.ds(base[q], 8), :], window)
                base_l = by_lane(lane, depth, [b.astype(jnp.float32) for b in base])
                target = (first * inverse_l + offset_l) - base_l + fine
                lower = target.astype(jnp.int32)
                frac = target - lower.astype(jnp.float32)
                left = rows_at(window, lower)
                return left + frac * (rows_at(window, lower + 1) - left)

            def sixteen(i, carry):
                pair = jnp.concatenate([eight(2 * i), eight(2 * i + 1)], axis=0)
                at = pl.ds(pl.multiple_of(16 * i, 16), 16)
                high[at, :], low[at, :] = two_parts(pair)
                return carry

            lax.fori_loop(0, width // 16, sixteen, 0, unroll=4)
            shift_l = by_lane(wide_lane, depth, shift)
            hits = (place - HALO - shift_l == (wide_lane & (depth - 1))) & keep
            select = jnp.where(hits, 1.0, 0.0).astype(jnp.bfloat16)
            total += lax.dot_general(select, high[...], NT, preferred_element_type=jnp.float32)
            total += lax.dot_general(select, low[...], NT, preferred_element_type=jnp.float32)
        proj[j] = total
        return carry

    lax.fori_loop(0, half, angle, 0)
    for j in range(half):
        up[8 * j : 8 * j + 8, :] = proj[j, depth : depth + 8, :]
        down[8 * j : 8 * j + 8, :] = proj[j, :8, :]
        at = 8 * half + HALO * j
        up[at : at + HALO, :] = measured[j][depth - HALO :, :]
        down[at : at + HALO, :] = measured[j][:HALO, :]
        sums[j : j + 1, :] = jnp.sum(proj[j], axis=0, keepdims=True)
        sums[half + j : half + j + 1, :] = jnp.sum(measured[j][...], axis=0, keepdims=True)
    at = (8 + HALO) * half
    up[at:, :] = sums[...]
    down[at:, :] = sums[...]


def backward_kernel(n, depth, width, slabs, *refs):
    half = n // 2
    info, own_table, other_table, proj, sums, from_below, from_above = refs[:7]
    others, measured = refs[7 : 7 + slabs - 3], refs[7 + slabs - 3 : 7 + slabs - 3 + half]
    residual, own, other = refs[7 + slabs - 3 + half : 10 + slabs - 3 + half]
    held, stack, turned, high, low, table, sem = refs[10 + slabs - 3 + half :]
    tiles = width // LANES
    per = LANES // depth
    groups = half // per
    rows = depth + 2 * HALO
    centre = (width - 1) / 2.0
    pad = 24
    band, slab = info[0], info[1]
    copies = copy_tables((own_table, other_table), tiles * depth, table, sem)
    edge = (8 + HALO) * half
    column = sums[...] + from_below[edge:, :] + from_above[edge:, :]
    for ref in others:
        column += ref[...]
    place = lax.broadcasted_iota(jnp.int32, (rows, width), 0)
    keep = (place >= HALO) | (slab > 0)
    keep = keep & ((place < HALO + depth) | (slab < slabs - 1))
    for j in range(half):
        gain = column[half + j : half + j + 1, :] / column[j : j + 1, :]
        at = 8 * half + HALO * j
        wanted = jnp.concatenate(
            [from_below[at : at + HALO, :], measured[j][...], from_above[at : at + HALO, :]], axis=0
        )
        image = jnp.concatenate(
            [
                proj[j, :8, :] + from_below[8 * j : 8 * j + 8, :],
                proj[j, 8:depth, :],
                proj[j, depth:, :] + from_above[8 * j : 8 * j + 8, :],
            ],
            axis=0,
        )
        value = jnp.where(keep, (wanted - gain * image) * (1.0 / n), 0.0)
        if j == 0:
            residual[...] = value[HALO : HALO + depth, :]
        for tile in range(tiles):
            held[j, tile] = value[:, tile * LANES : (tile + 1) * LANES]
    for copy in copies:
        copy.wait()

    lane = lax.broadcasted_iota(jnp.int32, (8, LANES), 1)
    step = lax.broadcasted_iota(jnp.int32, (8, LANES), 0).astype(jnp.float32)
    place = lax.broadcasted_iota(jnp.int32, (depth, LANES), 0)
    wide_lane = lax.broadcasted_iota(jnp.int32, (depth, LANES), 1)
    select = jnp.where(place == (wide_lane & (depth - 1)), 1.0, 0.0).astype(jnp.bfloat16)
    turned[:pad, :] = jnp.zeros((pad, LANES), jnp.float32)
    turned[pad + width :, :] = jnp.zeros((pad, LANES), jnp.float32)

    for cell, out in enumerate((own, other)):
        total = jnp.zeros((depth, width), jnp.float32)
        for g in range(groups):
            angles = [band ^ (2 * (g * per + q)) for q in range(per)]
            inverse = [table[cell, 0, a] for a in angles]
            offset = [table[cell, 1, a] for a in angles]
            shift = [table[cell, 2, a].astype(jnp.int32) + HALO for a in angles]
            magnification = [table[cell, 3, a] for a in angles]
            for tile in range(tiles):
                for q in range(per):
                    stack[q * depth : (q + 1) * depth, :] = held[g * per + q, tile, pl.ds(shift[q], depth), :]
                turned[pad + tile * LANES : pad + (tile + 1) * LANES, :] = stack[...].T
            inverse_l = by_lane(lane, depth, inverse)
            offset_l = by_lane(lane, depth, offset)
            magnification_l = by_lane(lane, depth, magnification)
            fine = step * magnification_l

            def eight(block):
                first = (block * 8).astype(jnp.float32)
                base = [
                    jnp.clip(
                        ((first - offset[q]) * magnification[q] + (centre + 1024.0)).astype(jnp.int32) - 1025,
                        -pad,
                        width,
                    )
                    for q in range(per)
                ]
                windows = [turned[pl.ds(base[0] + (pad + 8 * r), 8), :] for r in range(3)]
                for q in range(1, per):
                    here = lane >= q * depth
                    windows = [
                        jnp.where(here, turned[pl.ds(base[q] + (pad + 8 * r), 8), :], windows[r]) for r in range(3)
                    ]
                base_l = by_lane(lane, depth, [b.astype(jnp.float32) for b in base])
                target = ((first - offset_l) * magnification_l + centre) - base_l + fine
                lower = target.astype(jnp.int32)
                frac = target - lower.astype(jnp.float32)
                out = jnp.zeros((8, LANES), jnp.float32)
                for tap in range(4):
                    index = lower + (tap - 1)
                    within = index & 7
                    value = jnp.where(index < 8, rows_at(windows[0], within), rows_at(windows[1], within))
                    if tap >= 2:
                        value = jnp.where(index < 16, value, rows_at(windows[2], within))
                    weight = jnp.maximum(0.0, 1.0 - jnp.abs((frac + (1.0 - tap)) * inverse_l))
                    out += weight * value
                return out

            def sixteen(i, carry):
                pair = jnp.concatenate([eight(2 * i), eight(2 * i + 1)], axis=0)
                at = pl.ds(pl.multiple_of(16 * i, 16), 16)
                high[at, :], low[at, :] = two_parts(pair)
                return carry

            lax.fori_loop(0, width // 16, sixteen, 0, unroll=2)
            total += lax.dot_general(select, high[...], NT, preferred_element_type=jnp.float32)
            total += lax.dot_general(select, low[...], NT, preferred_element_type=jnp.float32)
        out[...] = total * (1.0 / math.sqrt(n))


def swapped(x, by):
    n = lax.axis_size("xband")
    return lax.ppermute(x, "xband", [(i, i ^ by) for i in range(n)])


def from_slab(x, by):
    n = lax.axis_size("zslab")
    return lax.ppermute(x, "zslab", [(i, (i + by) % n) for i in range(n)])


def shards(volume, measured, magnification, shift_y, shift_z):
    _, depth, width = volume.shape
    n, slabs = lax.axis_size("xband"), lax.axis_size("zslab")
    half = n // 2
    rows = depth + 2 * HALO
    centre = (width - 1) / 2.0
    f32 = jnp.float32
    info = jnp.stack([lax.axis_index("xband"), lax.axis_index("zslab")]).astype(jnp.int32)

    mag = magnification[:, 0]
    entries = jnp.stack(
        [1.0 / mag, centre + shift_y[:, 0].astype(f32), shift_z[:, 0].astype(f32), mag], axis=0
    )
    entries = jnp.pad(entries, ((0, 4), (0, LANES - n)))
    packed = volume[0].reshape(depth, width // LANES, LANES).transpose(1, 0, 2).reshape(-1, LANES)
    packed = jnp.concatenate([packed, entries], axis=0)

    mine = [packed] + [swapped(packed, 2 * k) for k in range(1, half)]
    views = [measured[0]] + [swapped(measured[0], 2 * k) for k in range(1, half)]
    theirs = [swapped(x, 1) for x in mine]

    smem = pl.BlockSpec(memory_space=pltpu.SMEM)
    vmem = pl.BlockSpec(memory_space=pltpu.VMEM)
    edge_rows = (8 + HALO + 2) * half
    params = pltpu.CompilerParams(vmem_limit_bytes=VMEM_LIMIT)
    proj, up, down, sums = pl.pallas_call(
        functools.partial(forward_kernel, n, depth, width, slabs),
        out_shape=[
            jax.ShapeDtypeStruct((half, rows, width), f32),
            jax.ShapeDtypeStruct((edge_rows, width), f32),
            jax.ShapeDtypeStruct((edge_rows, width), f32),
            jax.ShapeDtypeStruct((2 * half, width), f32),
        ],
        in_specs=[smem] + [vmem] * (n + half),
        out_specs=[vmem] * 4,
        scratch_shapes=[
            pltpu.VMEM((n * depth // LANES, width, LANES), f32),
            pltpu.VMEM((width, LANES), jnp.bfloat16),
            pltpu.VMEM((width, LANES), jnp.bfloat16),
            pltpu.SMEM((n, 8, LANES), f32),
            pltpu.SemaphoreType.DMA((n,)),
        ],
        compiler_params=params,
    )(info, *mine, *theirs, *views)

    from_below, from_above = from_slab(up, 1), from_slab(down, -1)
    others = [from_slab(sums, k) for k in range(2, slabs - 1)]

    residual, own, other = pl.pallas_call(
        functools.partial(backward_kernel, n, depth, width, slabs),
        out_shape=[jax.ShapeDtypeStruct((depth, width), f32)] * 3,
        in_specs=[smem] + [vmem] * (6 + len(others) + half),
        out_specs=[vmem] * 3,
        scratch_shapes=[
            pltpu.VMEM((half, width // LANES, rows, LANES), f32),
            pltpu.VMEM((LANES, LANES), f32),
            pltpu.VMEM((width + 48, LANES), f32),
            pltpu.VMEM((width, LANES), jnp.bfloat16),
            pltpu.VMEM((width, LANES), jnp.bfloat16),
            pltpu.SMEM((2, 8, LANES), f32),
            pltpu.SemaphoreType.DMA((2,)),
        ],
        compiler_params=params,
    )(info, mine[0], theirs[0], proj, sums, from_below, from_above, *others, *views)

    correction = own + swapped(other, 1)
    return residual[None], correction[None]


def solution(mesh):
    return jax.shard_map(
        shards,
        mesh=mesh,
        in_specs=(
            P("xband", "zslab", None),
            P("xband", "zslab", None),
            P(None, "xband"),
            P(None, "xband"),
            P(None, "xband"),
        ),
        out_specs=(P("xband", "zslab", None), P("xband", "zslab", None)),
        check_vma=False,
    )
```

```python
import functools
import math

import jax
import jax.numpy as jnp
from jax import lax
from jax.experimental import pallas as pl
from jax.experimental.pallas import tpu as pltpu
from jax.sharding import PartitionSpec as P

HALO = 4
LANES = 128
PAD = 24
Y_BITS = 21
U_BITS = 20
INVERSE, SHIFT, Y_STRIDE, Y_MIDDLE, U_STRIDE, U_MIDDLE, MAGNIFICATION = range(7)
VMEM_LIMIT = 48 * 1024 * 1024
NT = (((1,), (1,)), ((), ()))


def rows_at(tile, index):
    return jnp.take_along_axis(tile, index, axis=0, mode="promise_in_bounds")


def by_lane(lane, depth, values):
    out = jnp.full(lane.shape, values[0])
    for q in range(1, len(values)):
        out = jnp.where(lane >= q * depth, values[q], out)
    return out


def lanes_turned(tile, by):
    lane = lax.broadcasted_iota(jnp.int32, tile.shape, 1)
    return jnp.take_along_axis(tile, lane ^ by, axis=1, mode="promise_in_bounds")


def two_parts(x):
    high = x.astype(jnp.bfloat16)
    return high, (x - high.astype(jnp.float32)).astype(jnp.bfloat16)


def inside(shape, depth, slab, slabs):
    place = lax.broadcasted_iota(jnp.int32, shape, 0)
    return ((place >= HALO) | (slab > 0)) & ((place < HALO + depth) | (slab < slabs - 1))


def pack_kernel(depth, width, volume, magnification, shift_y, shift_z, place, packed, sem):
    tiles = width // LANES
    copies = [
        pltpu.make_async_copy(
            volume.at[:, pl.ds(tile * LANES, LANES)], packed.at[pl.ds(tile * depth, depth)], sem.at[tile]
        )
        for tile in range(tiles)
    ]
    for copy in copies:
        copy.start()
    mag = magnification[...]
    n = mag.shape[1]
    offset = (width - 1) / 2.0 + shift_y[...].astype(jnp.float32)
    rows = [
        1.0 / mag,
        shift_z[...].astype(jnp.float32),
        jnp.round(8.0 * 2.0**Y_BITS / mag),
        jnp.round((0.5 / mag + offset) * 2.0**Y_BITS),
        jnp.round(8.0 * 2.0**U_BITS * mag),
        jnp.round(((width // 2 - offset) * mag + (width - 1) / 2.0) * 2.0**U_BITS),
        mag,
        mag,
    ]
    table = jnp.concatenate([jnp.concatenate(rows, axis=0), jnp.zeros((8, LANES - n), jnp.float32)], axis=1)
    packed[tiles * depth :, :] = lanes_turned(table, place[...])
    for copy in copies:
        copy.wait()


def edges_kernel(half, depth, *refs):
    proj, measured, (up, down, sums) = refs[0], refs[1 : 1 + half], refs[1 + half :]
    for j in range(half):
        up[8 * j : 8 * j + 8, :] = proj[j, depth : depth + 8, :]
        down[8 * j : 8 * j + 8, :] = proj[j, :8, :]
        at = 8 * half + HALO * j
        up[at : at + HALO, :] = measured[j][depth - HALO :, :]
        down[at : at + HALO, :] = measured[j][:HALO, :]
        sums[j : j + 1, :] = jnp.sum(proj[j], axis=0, keepdims=True)
        sums[half + j : half + j + 1, :] = jnp.sum(measured[j][...], axis=0, keepdims=True)
    at = (8 + HALO) * half
    up[at:, :] = sums[...]
    down[at:, :] = sums[...]


def forward_kernel(half, depth, width, slabs, bands, swap, added, *refs):
    info, volumes = refs[0], refs[1 : 1 + bands]
    before = refs[1 + bands] if added else None
    proj, turned, images = refs[1 + bands + added :]
    tiles = width // LANES
    per = LANES // depth
    groups = bands // per
    rows = depth + 2 * HALO
    slab = info[1]
    for g in range(groups):
        for tile in range(tiles):
            part = slice(tile * depth, (tile + 1) * depth)
            block = jnp.concatenate([volumes[g * per + q][part, :] for q in range(per)], axis=0)
            turned[g, tile * LANES : (tile + 1) * LANES, :] = block.T

    lane = lax.broadcasted_iota(jnp.int32, (8, LANES), 1)
    step = lax.broadcasted_iota(jnp.int32, (8, LANES), 0).astype(jnp.float32)
    place = lax.broadcasted_iota(jnp.int32, (rows, LANES), 0)
    wide_lane = lax.broadcasted_iota(jnp.int32, (rows, LANES), 1)
    keep = inside((rows, LANES), depth, slab, slabs)
    together = images.shape[0]

    def gather(i, g, inverse, stride, start):
        fine = step * by_lane(lane, depth, inverse)
        stride_l = by_lane(lane, depth, stride)
        start_l = by_lane(lane, depth, start)

        def eight(point, point_l):
            window = turned[g, pl.ds(point[0] >> Y_BITS, 8), :]
            for q in range(1, per):
                window = jnp.where(lane >= q * depth, turned[g, pl.ds(point[q] >> Y_BITS, 8), :], window)
            target = (point_l & (2**Y_BITS - 1)).astype(jnp.float32) * 2.0**-Y_BITS + fine
            lower = target.astype(jnp.int32)
            frac = target - lower.astype(jnp.float32)
            left = rows_at(window, lower)
            return left + frac * (rows_at(window, lower + 1) - left)

        def sixteen(block, carry):
            point, point_l = carry
            first = eight(point, point_l)
            point, point_l = [p + d for p, d in zip(point, stride)], point_l + stride_l
            pair = jnp.concatenate([first, eight(point, point_l)], axis=0)
            point, point_l = [p + d for p, d in zip(point, stride)], point_l + stride_l
            at = pl.ds(pl.multiple_of(16 * block, 16), 16)
            images[i, g, at, :LANES], images[i, g, at, LANES:] = two_parts(pair)
            return point, point_l

        lax.fori_loop(0, width // 16, sixteen, (start, start_l), unroll=8)

    def some_angles(first, carry):
        tables, whole = [], []
        for k in range(bands):
            table = volumes[k][tiles * depth :, :]
            if together < half:
                table = lanes_turned(table, first * (2 * together))
            tables.append(table)
            numbers = table.astype(jnp.int32)
            ahead = pltpu.roll(numbers, Y_MIDDLE - Y_STRIDE, 0)
            here = lax.broadcasted_iota(jnp.int32, (8, LANES), 0)
            whole.append(jnp.where(here == Y_MIDDLE, numbers - (width // 16) * ahead, numbers))

        def value(source, row, i):
            return [[source[g * per + q][row, 2 * ((g * per + q) ^ i) + swap] for q in range(per)] for g in range(groups)]

        scalars = [
            [value(tables, INVERSE, i), value(whole, Y_STRIDE, i), value(whole, Y_MIDDLE, i), value(whole, SHIFT, i)]
            for i in range(together)
        ]
        for i in range(together):
            for g in range(groups):
                gather(i, g, *[entry[g] for entry in scalars[i][:3]])
        for i in range(together):
            j = first * together + i
            total = before[j] if added else None
            for g in range(groups):
                shift_l = by_lane(wide_lane, depth, scalars[i][3][g])
                hits = (place - HALO - shift_l == (wide_lane & (depth - 1))) & keep
                select = jnp.where(hits, 1.0, 0.0).astype(jnp.bfloat16)
                select = jnp.concatenate([select, select], axis=1)
                image = lax.dot_general(select, images[i, g], NT, preferred_element_type=jnp.float32)
                total = image if total is None else total + image
            proj[j] = total
        return carry

    if together == half:
        some_angles(0, 0)
    else:
        lax.fori_loop(0, half // together, some_angles, 0)


def project_back(half, depth, width, swap, entries, held, out, stack, turned, images):
    tiles = width // LANES
    per = LANES // depth
    groups = half // per
    lane = lax.broadcasted_iota(jnp.int32, (8, LANES), 1)
    step = lax.broadcasted_iota(jnp.int32, (8, LANES), 0).astype(jnp.float32)
    place = lax.broadcasted_iota(jnp.int32, (depth, LANES), 0)
    wide_lane = lax.broadcasted_iota(jnp.int32, (depth, LANES), 1)
    select = jnp.where(place == (wide_lane & (depth - 1)), 1.0, 0.0).astype(jnp.bfloat16)
    select = jnp.concatenate([select, select], axis=1)
    turned[:PAD, :] = jnp.zeros((PAD, LANES), jnp.float32)
    turned[PAD + width :, :] = jnp.zeros((PAD, LANES), jnp.float32)
    table = entries[tiles * depth :, :]
    numbers = table.astype(jnp.int32)
    ahead = pltpu.roll(numbers, U_MIDDLE - U_STRIDE, 0)
    here = lax.broadcasted_iota(jnp.int32, (8, LANES), 0)
    numbers = jnp.where(here == U_MIDDLE, numbers - (width // 16) * ahead, numbers)

    def value(source, row, g):
        return [source[row, 2 * (g * per + q) + swap] for q in range(per)]

    total = jnp.zeros((depth, width), jnp.float32)
    for g in range(groups):
        shift = [d + HALO for d in value(numbers, SHIFT, g)]
        stride, start = value(numbers, U_STRIDE, g), value(numbers, U_MIDDLE, g)
        for tile in range(tiles):
            for q in range(per):
                stack[tile, q * depth : (q + 1) * depth, :] = held[g * per + q, tile, pl.ds(shift[q], depth), :]
            turned[PAD + tile * LANES : PAD + (tile + 1) * LANES, :] = stack[tile].T
        inverse_l = by_lane(lane, depth, value(table, INVERSE, g))
        fine = step * by_lane(lane, depth, value(table, MAGNIFICATION, g))
        stride_l = by_lane(lane, depth, stride)
        start_l = by_lane(lane, depth, start)

        def eight(point, point_l):
            base = [jnp.clip((p >> U_BITS) - 1, -PAD, width) + PAD for p in point]
            windows = [turned[pl.ds(base[0] + 8 * r, 8), :] for r in range(3)]
            for q in range(1, per):
                here = lane >= q * depth
                windows = [jnp.where(here, turned[pl.ds(base[q] + 8 * r, 8), :], windows[r]) for r in range(3)]
            target = (point_l & (2**U_BITS - 1)).astype(jnp.float32) * 2.0**-U_BITS + fine
            lower = target.astype(jnp.int32)
            frac = (target - lower.astype(jnp.float32)) * inverse_l
            out = jnp.zeros((8, LANES), jnp.float32)
            for tap in range(4):
                index = lower + tap
                within = index & 7
                value = jnp.where(index < 8, rows_at(windows[0], within), rows_at(windows[1], within))
                if tap >= 2:
                    value = jnp.where(index < 16, value, rows_at(windows[2], within))
                weight = jnp.maximum(0.0, 1.0 - jnp.abs(frac + (1.0 - tap) * inverse_l))
                out += weight * value
            return out

        def sixteen(i, carry):
            point, point_l = carry
            first = eight(point, point_l)
            point, point_l = [p + d for p, d in zip(point, stride)], point_l + stride_l
            pair = jnp.concatenate([first, eight(point, point_l)], axis=0)
            point, point_l = [p + d for p, d in zip(point, stride)], point_l + stride_l
            at = pl.ds(pl.multiple_of(16 * i, 16), 16)
            images[at, :LANES], images[at, LANES:] = two_parts(pair)
            return point, point_l

        lax.fori_loop(0, width // 16, sixteen, (start, start_l), unroll=4)
        total += lax.dot_general(select, images[...], NT, preferred_element_type=jnp.float32)
    out[...] = total * (1.0 / math.sqrt(2 * half))


def residual_kernel(half, depth, width, slabs, *refs):
    info, entries, proj, sums, from_below, from_above = refs[:6]
    others, measured = refs[6 : 6 + slabs - 3], refs[6 + slabs - 3 : 6 + slabs - 3 + half]
    residual, held, other, stack, turned, images = refs[6 + slabs - 3 + half :]
    rows = depth + 2 * HALO
    tiles = width // LANES
    edge = (8 + HALO) * half
    column = sums[...] + from_below[edge:, :] + from_above[edge:, :]
    for ref in others:
        column += ref[...]
    keep = inside((rows, LANES), depth, info[1], slabs)
    for j in range(half):
        at = 8 * half + HALO * j
        for tile in range(tiles):
            part = slice(tile * LANES, (tile + 1) * LANES)
            image = jnp.concatenate(
                [
                    proj[j, :8, part] + from_below[8 * j : 8 * j + 8, part],
                    proj[j, 8:depth, part],
                    proj[j, depth:, part] + from_above[8 * j : 8 * j + 8, part],
                ],
                axis=0,
            )
            wanted = jnp.concatenate(
                [from_below[at : at + HALO, part], measured[j][:, part], from_above[at : at + HALO, part]], axis=0
            )
            gain = column[half + j : half + j + 1, part] / column[j : j + 1, part]
            value = jnp.where(keep, (wanted - gain * image) * (1.0 / (2 * half)), 0.0)
            if j == 0:
                residual[:, part] = value[HALO : HALO + depth, :]
            held[j, tile] = value
    project_back(half, depth, width, 1, entries, held, other, stack, turned, images)


def own_kernel(half, depth, width, entries, held, out, stack, turned, images):
    project_back(half, depth, width, 0, entries, held, out, stack, turned, images)


def swapped(x, by):
    n = lax.axis_size("xband")
    return lax.ppermute(x, "xband", [(i, i ^ by) for i in range(n)])


def from_slab(x, by):
    n = lax.axis_size("zslab")
    return lax.ppermute(x, "zslab", [(i, (i + by) % n) for i in range(n)])


def shards(volume, measured, magnification, shift_y, shift_z):
    _, depth, width = volume.shape
    n, slabs = lax.axis_size("xband"), lax.axis_size("zslab")
    half = n // 2
    rows = depth + 2 * HALO
    tiles = width // LANES
    f32, bf16 = jnp.float32, jnp.bfloat16
    info = jnp.stack([lax.axis_index("xband"), lax.axis_index("zslab")]).astype(jnp.int32)

    smem = pl.BlockSpec(memory_space=pltpu.SMEM)
    vmem = pl.BlockSpec(memory_space=pltpu.VMEM)
    params = pltpu.CompilerParams(vmem_limit_bytes=VMEM_LIMIT)

    def on_core(body, shapes, operands, scratch=(), spaces={}):
        out = pl.pallas_call(
            body,
            out_shape=[jax.ShapeDtypeStruct(shape, f32) for shape in shapes],
            in_specs=[spaces.get(i, smem if x is info else vmem) for i, x in enumerate(operands)],
            out_specs=[vmem] * len(shapes),
            scratch_shapes=scratch,
            compiler_params=params,
        )(*operands)
        return out if len(shapes) > 1 else out[0]

    place = jnp.full((1, 1), lax.axis_index("xband"), jnp.int32)
    packed = on_core(
        functools.partial(pack_kernel, depth, width),
        [(tiles * depth + 8, LANES)],
        [volume[0]] + [x.reshape(1, n) for x in (magnification, shift_y, shift_z)] + [place],
        [pltpu.SemaphoreType.DMA((tiles,))],
        {0: pl.BlockSpec(memory_space=pl.ANY)},
    )
    far_first = range(half - 1, 0, -1)
    moved = {k: swapped(packed, 2 * k) for k in far_first}
    mine = [packed] + [moved[k] for k in range(1, half)]
    first_swap = swapped(packed, 1)

    view, first_swap = lax.optimization_barrier((measured[0], first_swap))
    moved = {k: swapped(view, 2 * k) for k in far_first}
    views = [view] + [moved[k] for k in range(1, half)]
    theirs = [first_swap] + [swapped(x, 1) for x in mine[1:]]

    def forward(volumes, swap, before):
        bands = len(volumes)
        return on_core(
            functools.partial(forward_kernel, half, depth, width, slabs, bands, swap, len(before)),
            [(half, rows, width)],
            [info] + volumes + before,
            [
                pltpu.VMEM((bands * depth // LANES, width, LANES), f32),
                pltpu.VMEM((min(half, 4), bands * depth // LANES, width, 2 * LANES), bf16),
            ],
        )

    proj = forward(theirs, 1, [forward(mine, 0, [])])
    edge_rows = (8 + HALO + 2) * half
    up, down, sums = on_core(
        functools.partial(edges_kernel, half, depth),
        [(edge_rows, width), (edge_rows, width), (2 * half, width)],
        [proj] + views,
    )
    below, above = from_slab(up, 1), from_slab(down, -1)
    others = [from_slab(sums, k) for k in range(2, slabs - 1)]

    scratch = [
        pltpu.VMEM((tiles, LANES, LANES), f32),
        pltpu.VMEM((width + 2 * PAD, LANES), f32),
        pltpu.VMEM((width, 2 * LANES), bf16),
    ]
    residual, held, other = on_core(
        functools.partial(residual_kernel, half, depth, width, slabs),
        [(depth, width), (half, tiles, rows, LANES), (depth, width)],
        [info, theirs[0], proj, sums, below, above] + others + views,
        scratch,
    )
    from_other = swapped(other, 1)
    own = on_core(
        functools.partial(own_kernel, half, depth, width), [(depth, width)], [mine[0], held], scratch
    )
    return residual[None], (own + from_other)[None]


def solution(mesh):
    return jax.shard_map(
        shards,
        mesh=mesh,
        in_specs=(
            P("xband", "zslab", None),
            P("xband", "zslab", None),
            P(None, "xband"),
            P(None, "xband"),
            P(None, "xband"),
        ),
        out_specs=(P("xband", "zslab", None), P("xband", "zslab", None)),
        check_vma=False,
    )
```

```python
import functools
import math

import jax
import jax.numpy as jnp
from jax import lax
from jax.experimental import pallas as pl
from jax.experimental.pallas import tpu as pltpu
from jax.sharding import PartitionSpec as P

HALO = 4
LANES = 128
PAD = 24
Y_BITS = 21
U_BITS = 20
INVERSE, SHIFT, Y_STRIDE, Y_MIDDLE, U_STRIDE, U_MIDDLE, MAGNIFICATION = range(7)
VMEM_LIMIT = 48 * 1024 * 1024
NT = (((1,), (1,)), ((), ()))


def rows_at(tile, index):
    return jnp.take_along_axis(tile, index, axis=0, mode="promise_in_bounds")


def by_lane(lane, depth, values):
    out = jnp.full(lane.shape, values[0])
    for q in range(1, len(values)):
        out = jnp.where(lane >= q * depth, values[q], out)
    return out


def lanes_turned(tile, by):
    lane = lax.broadcasted_iota(jnp.int32, tile.shape, 1)
    return jnp.take_along_axis(tile, lane ^ by, axis=1, mode="promise_in_bounds")


def two_parts(x):
    high = x.astype(jnp.bfloat16)
    return high, (x - high.astype(jnp.float32)).astype(jnp.bfloat16)


def inside(shape, depth, slab, slabs):
    place = lax.broadcasted_iota(jnp.int32, shape, 0)
    return ((place >= HALO) | (slab > 0)) & ((place < HALO + depth) | (slab < slabs - 1))


def pack_kernel(depth, width, volume, *refs):
    small, place, packed, held, sem = refs[:3], refs[3], refs[4], refs[5:8], refs[8]
    magnification, shift_y, shift_z = held
    tiles = width // LANES
    small_copies = [pltpu.make_async_copy(x, y, sem.at[tiles + i]) for i, (x, y) in enumerate(zip(small, held))]
    for copy in small_copies:
        copy.start()
    copies = [
        pltpu.make_async_copy(
            volume.at[:, pl.ds(tile * LANES, LANES)], packed.at[pl.ds(tile * depth, depth)], sem.at[tile]
        )
        for tile in range(tiles)
    ]
    for copy in copies:
        copy.start()
    for copy in small_copies:
        copy.wait()
    mag = magnification[...]
    n = mag.shape[1]
    offset = (width - 1) / 2.0 + shift_y[...].astype(jnp.float32)
    rows = [
        1.0 / mag,
        shift_z[...].astype(jnp.float32),
        jnp.round(8.0 * 2.0**Y_BITS / mag),
        jnp.round((0.5 / mag + offset) * 2.0**Y_BITS),
        jnp.round(8.0 * 2.0**U_BITS * mag),
        jnp.round(((width // 2 - offset) * mag + (width - 1) / 2.0) * 2.0**U_BITS),
        mag,
        mag,
    ]
    table = jnp.concatenate([jnp.concatenate(rows, axis=0), jnp.zeros((8, LANES - n), jnp.float32)], axis=1)
    packed[tiles * depth :, :] = lanes_turned(table, place[...])
    for copy in copies:
        copy.wait()


def edges_kernel(half, depth, *refs):
    proj, measured, (up, down, sums) = refs[0], refs[1 : 1 + half], refs[1 + half :]
    for j in range(half):
        up[8 * j : 8 * j + 8, :] = proj[j, depth : depth + 8, :]
        down[8 * j : 8 * j + 8, :] = proj[j, :8, :]
        at = 8 * half + HALO * j
        up[at : at + HALO, :] = measured[j][depth - HALO :, :]
        down[at : at + HALO, :] = measured[j][:HALO, :]
        sums[j : j + 1, :] = jnp.sum(proj[j], axis=0, keepdims=True)
        sums[half + j : half + j + 1, :] = jnp.sum(measured[j][...], axis=0, keepdims=True)
    at = (8 + HALO) * half
    up[at:, :] = sums[...]
    down[at:, :] = sums[...]


def forward_kernel(half, depth, width, slabs, bands, swap, added, *refs):
    info, volumes = refs[0], refs[1 : 1 + bands]
    before = refs[1 + bands] if added else None
    proj, turned, images = refs[1 + bands + added :]
    tiles = width // LANES
    per = LANES // depth
    groups = bands // per
    rows = depth + 2 * HALO
    slab = info[1]
    for g in range(groups):
        for tile in range(tiles):
            part = slice(tile * depth, (tile + 1) * depth)
            block = jnp.concatenate([volumes[g * per + q][part, :] for q in range(per)], axis=0)
            turned[g, tile * LANES : (tile + 1) * LANES, :] = block.T

    lane = lax.broadcasted_iota(jnp.int32, (8, LANES), 1)
    step = lax.broadcasted_iota(jnp.int32, (8, LANES), 0).astype(jnp.float32)
    place = lax.broadcasted_iota(jnp.int32, (rows, LANES), 0)
    wide_lane = lax.broadcasted_iota(jnp.int32, (rows, LANES), 1)
    keep = inside((rows, LANES), depth, slab, slabs)
    together = images.shape[0]

    def gather(i, g, inverse, stride, start):
        fine = step * by_lane(lane, depth, inverse)
        stride_l = by_lane(lane, depth, stride)
        start_l = by_lane(lane, depth, start)

        def eight(point, point_l):
            window = turned[g, pl.ds(point[0] >> Y_BITS, 8), :]
            for q in range(1, per):
                window = jnp.where(lane >= q * depth, turned[g, pl.ds(point[q] >> Y_BITS, 8), :], window)
            target = (point_l & (2**Y_BITS - 1)).astype(jnp.float32) * 2.0**-Y_BITS + fine
            lower = target.astype(jnp.int32)
            frac = target - lower.astype(jnp.float32)
            left = rows_at(window, lower)
            return left + frac * (rows_at(window, lower + 1) - left)

        def sixteen(block, carry):
            point, point_l = carry
            first = eight(point, point_l)
            point, point_l = [p + d for p, d in zip(point, stride)], point_l + stride_l
            pair = jnp.concatenate([first, eight(point, point_l)], axis=0)
            point, point_l = [p + d for p, d in zip(point, stride)], point_l + stride_l
            at = pl.ds(pl.multiple_of(16 * block, 16), 16)
            images[i, g, at, :LANES], images[i, g, at, LANES:] = two_parts(pair)
            return point, point_l

        lax.fori_loop(0, width // 16, sixteen, (start, start_l), unroll=8)

    def some_angles(first, carry):
        tables, whole = [], []
        for k in range(bands):
            table = volumes[k][tiles * depth :, :]
            if together < half:
                table = lanes_turned(table, first * (2 * together))
            tables.append(table)
            numbers = table.astype(jnp.int32)
            ahead = pltpu.roll(numbers, Y_MIDDLE - Y_STRIDE, 0)
            here = lax.broadcasted_iota(jnp.int32, (8, LANES), 0)
            whole.append(jnp.where(here == Y_MIDDLE, numbers - (width // 16) * ahead, numbers))

        def value(source, row, i):
            return [[source[g * per + q][row, 2 * ((g * per + q) ^ i) + swap] for q in range(per)] for g in range(groups)]

        scalars = [
            [value(tables, INVERSE, i), value(whole, Y_STRIDE, i), value(whole, Y_MIDDLE, i), value(whole, SHIFT, i)]
            for i in range(together)
        ]
        for i in range(together):
            for g in range(groups):
                gather(i, g, *[entry[g] for entry in scalars[i][:3]])
        for i in range(together):
            j = first * together + i
            total = before[j] if added else None
            for g in range(groups):
                shift_l = by_lane(wide_lane, depth, scalars[i][3][g])
                hits = (place - HALO - shift_l == (wide_lane & (depth - 1))) & keep
                select = jnp.where(hits, 1.0, 0.0).astype(jnp.bfloat16)
                select = jnp.concatenate([select, select], axis=1)
                image = lax.dot_general(select, images[i, g], NT, preferred_element_type=jnp.float32)
                total = image if total is None else total + image
            proj[j] = total
        return carry

    if together == half:
        some_angles(0, 0)
    else:
        lax.fori_loop(0, half // together, some_angles, 0)


def project_back(half, depth, width, swap, entries, held, out, stack, turned, images):
    tiles = width // LANES
    per = LANES // depth
    groups = half // per
    lane = lax.broadcasted_iota(jnp.int32, (8, LANES), 1)
    step = lax.broadcasted_iota(jnp.int32, (8, LANES), 0).astype(jnp.float32)
    place = lax.broadcasted_iota(jnp.int32, (depth, LANES), 0)
    wide_lane = lax.broadcasted_iota(jnp.int32, (depth, LANES), 1)
    select = jnp.where(place == (wide_lane & (depth - 1)), 1.0, 0.0).astype(jnp.bfloat16)
    select = jnp.concatenate([select, select], axis=1)
    turned[:PAD, :] = jnp.zeros((PAD, LANES), jnp.float32)
    turned[PAD + width :, :] = jnp.zeros((PAD, LANES), jnp.float32)
    table = entries[tiles * depth :, :]
    numbers = table.astype(jnp.int32)
    ahead = pltpu.roll(numbers, U_MIDDLE - U_STRIDE, 0)
    here = lax.broadcasted_iota(jnp.int32, (8, LANES), 0)
    numbers = jnp.where(here == U_MIDDLE, numbers - (width // 16) * ahead, numbers)

    def value(source, row, g):
        return [source[row, 2 * (g * per + q) + swap] for q in range(per)]

    total = jnp.zeros((depth, width), jnp.float32)
    for g in range(groups):
        shift = [d + HALO for d in value(numbers, SHIFT, g)]
        stride, start = value(numbers, U_STRIDE, g), value(numbers, U_MIDDLE, g)
        for tile in range(tiles):
            for q in range(per):
                stack[tile, q * depth : (q + 1) * depth, :] = held[g * per + q, tile, pl.ds(shift[q], depth), :]
            turned[PAD + tile * LANES : PAD + (tile + 1) * LANES, :] = stack[tile].T
        inverse_l = by_lane(lane, depth, value(table, INVERSE, g))
        fine = step * by_lane(lane, depth, value(table, MAGNIFICATION, g))
        stride_l = by_lane(lane, depth, stride)
        start_l = by_lane(lane, depth, start)

        def eight(point, point_l):
            base = [jnp.clip((p >> U_BITS) - 1, -PAD, width) + PAD for p in point]
            windows = [turned[pl.ds(base[0] + 8 * r, 8), :] for r in range(3)]
            for q in range(1, per):
                here = lane >= q * depth
                windows = [jnp.where(here, turned[pl.ds(base[q] + 8 * r, 8), :], windows[r]) for r in range(3)]
            target = (point_l & (2**U_BITS - 1)).astype(jnp.float32) * 2.0**-U_BITS + fine
            lower = target.astype(jnp.int32)
            frac = (target - lower.astype(jnp.float32)) * inverse_l
            out = jnp.zeros((8, LANES), jnp.float32)
            for tap in range(4):
                index = lower + tap
                within = index & 7
                value = jnp.where(index < 8, rows_at(windows[0], within), rows_at(windows[1], within))
                if tap >= 2:
                    value = jnp.where(index < 16, value, rows_at(windows[2], within))
                weight = jnp.maximum(0.0, 1.0 - jnp.abs(frac + (1.0 - tap) * inverse_l))
                out += weight * value
            return out

        def sixteen(i, carry):
            point, point_l = carry
            first = eight(point, point_l)
            point, point_l = [p + d for p, d in zip(point, stride)], point_l + stride_l
            pair = jnp.concatenate([first, eight(point, point_l)], axis=0)
            point, point_l = [p + d for p, d in zip(point, stride)], point_l + stride_l
            at = pl.ds(pl.multiple_of(16 * i, 16), 16)
            images[at, :LANES], images[at, LANES:] = two_parts(pair)
            return point, point_l

        lax.fori_loop(0, width // 16, sixteen, (start, start_l), unroll=4)
        total += lax.dot_general(select, images[...], NT, preferred_element_type=jnp.float32)
    out[...] = total * (1.0 / math.sqrt(2 * half))


def residual_kernel(half, depth, width, slabs, *refs):
    info, entries, proj, sums, from_below, from_above = refs[:6]
    others, measured = refs[6 : 6 + slabs - 3], refs[6 + slabs - 3 : 6 + slabs - 3 + half]
    residual, held, other, stack, turned, images = refs[6 + slabs - 3 + half :]
    rows = depth + 2 * HALO
    tiles = width // LANES
    edge = (8 + HALO) * half
    column = sums[...] + from_below[edge:, :] + from_above[edge:, :]
    for ref in others:
        column += ref[...]
    keep = inside((rows, LANES), depth, info[1], slabs)
    for j in range(half):
        at = 8 * half + HALO * j
        for tile in range(tiles):
            part = slice(tile * LANES, (tile + 1) * LANES)
            image = jnp.concatenate(
                [
                    proj[j, :8, part] + from_below[8 * j : 8 * j + 8, part],
                    proj[j, 8:depth, part],
                    proj[j, depth:, part] + from_above[8 * j : 8 * j + 8, part],
                ],
                axis=0,
            )
            wanted = jnp.concatenate(
                [from_below[at : at + HALO, part], measured[j][:, part], from_above[at : at + HALO, part]], axis=0
            )
            gain = column[half + j : half + j + 1, part] / column[j : j + 1, part]
            value = jnp.where(keep, (wanted - gain * image) * (1.0 / (2 * half)), 0.0)
            if j == 0:
                residual[:, part] = value[HALO : HALO + depth, :]
            held[j, tile] = value
    project_back(half, depth, width, 1, entries, held, other, stack, turned, images)


def own_kernel(half, depth, width, entries, held, out, stack, turned, images):
    project_back(half, depth, width, 0, entries, held, out, stack, turned, images)


def swapped(x, by):
    n = lax.axis_size("xband")
    return lax.ppermute(x, "xband", [(i, i ^ by) for i in range(n)])


def from_slab(x, by):
    n = lax.axis_size("zslab")
    return lax.ppermute(x, "zslab", [(i, (i + by) % n) for i in range(n)])


def shards(volume, measured, magnification, shift_y, shift_z):
    _, depth, width = volume.shape
    n, slabs = lax.axis_size("xband"), lax.axis_size("zslab")
    half = n // 2
    rows = depth + 2 * HALO
    tiles = width // LANES
    f32, bf16 = jnp.float32, jnp.bfloat16
    info = jnp.stack([lax.axis_index("xband"), lax.axis_index("zslab")]).astype(jnp.int32)

    smem = pl.BlockSpec(memory_space=pltpu.SMEM)
    vmem = pl.BlockSpec(memory_space=pltpu.VMEM)
    params = pltpu.CompilerParams(vmem_limit_bytes=VMEM_LIMIT)

    def on_core(body, shapes, operands, scratch=(), spaces={}):
        out = pl.pallas_call(
            body,
            out_shape=[jax.ShapeDtypeStruct(shape, f32) for shape in shapes],
            in_specs=[spaces.get(i, smem if x is info else vmem) for i, x in enumerate(operands)],
            out_specs=[vmem] * len(shapes),
            scratch_shapes=scratch,
            compiler_params=params,
        )(*operands)
        return out if len(shapes) > 1 else out[0]

    place = jnp.full((1, 1), lax.axis_index("xband"), jnp.int32)
    packed = on_core(
        functools.partial(pack_kernel, depth, width),
        [(tiles * depth + 8, LANES)],
        [
            pltpu.with_memory_space_constraint(x, pltpu.HBM)
            for x in (volume[0], magnification.reshape(1, n), shift_y.reshape(1, n), shift_z.reshape(1, n))
        ]
        + [place],
        [
            pltpu.VMEM((1, n), f32),
            pltpu.VMEM((1, n), jnp.int32),
            pltpu.VMEM((1, n), jnp.int32),
            pltpu.SemaphoreType.DMA((tiles + 3,)),
        ],
        {i: pl.BlockSpec(memory_space=pl.ANY) for i in range(4)},
    )
    far_first = range(half - 1, 0, -1)
    moved = {k: swapped(packed, 2 * k) for k in far_first}
    mine = [packed] + [moved[k] for k in range(1, half)]
    first_swap = swapped(packed, 1)

    view, first_swap = lax.optimization_barrier((measured[0], first_swap))
    moved = {k: swapped(view, 2 * k) for k in far_first}
    views = [view] + [moved[k] for k in range(1, half)]
    theirs = [first_swap] + [swapped(x, 1) for x in mine[1:]]

    def forward(volumes, swap, before):
        bands = len(volumes)
        return on_core(
            functools.partial(forward_kernel, half, depth, width, slabs, bands, swap, len(before)),
            [(half, rows, width)],
            [info] + volumes + before,
            [
                pltpu.VMEM((bands * depth // LANES, width, LANES), f32),
                pltpu.VMEM((min(half, 4), bands * depth // LANES, width, 2 * LANES), bf16),
            ],
        )

    proj = forward(theirs, 1, [forward(mine, 0, [])])
    edge_rows = (8 + HALO + 2) * half
    up, down, sums = on_core(
        functools.partial(edges_kernel, half, depth),
        [(edge_rows, width), (edge_rows, width), (2 * half, width)],
        [proj] + views,
    )
    below, above = from_slab(up, 1), from_slab(down, -1)
    others = [from_slab(sums, k) for k in range(2, slabs - 1)]

    scratch = [
        pltpu.VMEM((tiles, LANES, LANES), f32),
        pltpu.VMEM((width + 2 * PAD, LANES), f32),
        pltpu.VMEM((width, 2 * LANES), bf16),
    ]
    residual, held, other = on_core(
        functools.partial(residual_kernel, half, depth, width, slabs),
        [(depth, width), (half, tiles, rows, LANES), (depth, width)],
        [info, theirs[0], proj, sums, below, above] + others + views,
        scratch,
    )
    from_other = swapped(other, 1)
    own = on_core(
        functools.partial(own_kernel, half, depth, width), [(depth, width)], [mine[0], held], scratch
    )
    return residual[None], (own + from_other)[None]


def solution(mesh):
    return jax.shard_map(
        shards,
        mesh=mesh,
        in_specs=(
            P("xband", "zslab", None),
            P("xband", "zslab", None),
            P(None, "xband"),
            P(None, "xband"),
            P(None, "xband"),
        ),
        out_specs=(P("xband", "zslab", None), P("xband", "zslab", None)),
        check_vma=False,
    )
```

```python
import functools
import math

import jax
import jax.numpy as jnp
from jax import lax
from jax.experimental import pallas as pl
from jax.experimental.pallas import tpu as pltpu
from jax.sharding import PartitionSpec as P

HALO = 4
LANES = 128
PAD = 24
Y_BITS = 21
U_BITS = 20
INVERSE, SHIFT, Y_STRIDE, Y_MIDDLE, U_STRIDE, U_MIDDLE, MAGNIFICATION = range(7)
VMEM_LIMIT = 48 * 1024 * 1024
NT = (((1,), (1,)), ((), ()))


def rows_at(tile, index):
    return jnp.take_along_axis(tile, index, axis=0, mode="promise_in_bounds")


def by_lane(lane, depth, values):
    out = jnp.full(lane.shape, values[0])
    for q in range(1, len(values)):
        out = jnp.where(lane >= q * depth, values[q], out)
    return out


def lanes_turned(tile, by):
    lane = lax.broadcasted_iota(jnp.int32, tile.shape, 1)
    return jnp.take_along_axis(tile, lane ^ by, axis=1, mode="promise_in_bounds")


def two_parts(x):
    high = x.astype(jnp.bfloat16)
    return high, (x - high.astype(jnp.float32)).astype(jnp.bfloat16)


def inside(shape, depth, slab, slabs):
    place = lax.broadcasted_iota(jnp.int32, shape, 0)
    return ((place >= HALO) | (slab > 0)) & ((place < HALO + depth) | (slab < slabs - 1))


def pack_kernel(depth, width, volume, *refs):
    small, place, packed, held, sem = refs[:3], refs[3], refs[4], refs[5:8], refs[8]
    magnification, shift_y, shift_z = held
    tiles = width // LANES
    small_copies = [pltpu.make_async_copy(x, y, sem.at[tiles + i]) for i, (x, y) in enumerate(zip(small, held))]
    for copy in small_copies:
        copy.start()
    copies = [
        pltpu.make_async_copy(
            volume.at[:, pl.ds(tile * LANES, LANES)], packed.at[pl.ds(tile * depth, depth)], sem.at[tile]
        )
        for tile in range(tiles)
    ]
    for copy in copies:
        copy.start()
    for copy in small_copies:
        copy.wait()
    mag = magnification[...]
    n = mag.shape[1]
    offset = (width - 1) / 2.0 + shift_y[...].astype(jnp.float32)
    rows = [
        1.0 / mag,
        shift_z[...].astype(jnp.float32),
        jnp.round(8.0 * 2.0**Y_BITS / mag),
        jnp.round((0.5 / mag + offset) * 2.0**Y_BITS),
        jnp.round(8.0 * 2.0**U_BITS * mag),
        jnp.round(((width // 2 - offset) * mag + (width - 1) / 2.0) * 2.0**U_BITS),
        mag,
        mag,
    ]
    table = jnp.concatenate([jnp.concatenate(rows, axis=0), jnp.zeros((8, LANES - n), jnp.float32)], axis=1)
    packed[tiles * depth :, :] = lanes_turned(table, place[...])
    for copy in copies:
        copy.wait()


def edges_kernel(half, depth, *refs):
    proj, measured, (up, down, sums) = refs[0], refs[1 : 1 + half], refs[1 + half :]
    for j in range(half):
        up[8 * j : 8 * j + 8, :] = proj[j, depth : depth + 8, :]
        down[8 * j : 8 * j + 8, :] = proj[j, :8, :]
        at = 8 * half + HALO * j
        up[at : at + HALO, :] = measured[j][depth - HALO :, :]
        down[at : at + HALO, :] = measured[j][:HALO, :]
        sums[j : j + 1, :] = jnp.sum(proj[j], axis=0, keepdims=True)
        sums[half + j : half + j + 1, :] = jnp.sum(measured[j][...], axis=0, keepdims=True)
    at = (8 + HALO) * half
    up[at:, :] = sums[...]
    down[at:, :] = sums[...]


def forward_kernel(half, depth, width, slabs, bands, swap, added, *refs):
    info, volumes = refs[0], refs[1 : 1 + bands]
    before = refs[1 + bands] if added else None
    proj, turned, images = refs[1 + bands + added :]
    tiles = width // LANES
    per = LANES // depth
    groups = bands // per
    rows = depth + 2 * HALO
    for g in range(groups):
        for tile in range(tiles):
            part = slice(tile * depth, (tile + 1) * depth)
            block = jnp.concatenate([volumes[g * per + q][part, :] for q in range(per)], axis=0)
            turned[g, tile * LANES : (tile + 1) * LANES, :] = block.T

    lane = lax.broadcasted_iota(jnp.int32, (8, LANES), 1)
    step = lax.broadcasted_iota(jnp.int32, (8, LANES), 0).astype(jnp.float32)
    place = lax.broadcasted_iota(jnp.int32, (rows, LANES), 0)
    wide_lane = lax.broadcasted_iota(jnp.int32, (rows, LANES), 1)
    keep = info[...] > 0.0
    together = images.shape[0]

    def gather(i, g, inverse, stride, start):
        fine = step * by_lane(lane, depth, inverse)
        stride_l = by_lane(lane, depth, stride)
        start_l = by_lane(lane, depth, start)

        def eight(point, point_l):
            window = turned[g, pl.ds(point[0] >> Y_BITS, 8), :]
            for q in range(1, per):
                window = jnp.where(lane >= q * depth, turned[g, pl.ds(point[q] >> Y_BITS, 8), :], window)
            target = (point_l & (2**Y_BITS - 1)).astype(jnp.float32) * 2.0**-Y_BITS + fine
            lower = target.astype(jnp.int32)
            frac = target - lower.astype(jnp.float32)
            left = rows_at(window, lower)
            return left + frac * (rows_at(window, lower + 1) - left)

        def sixteen(block, carry):
            point, point_l = carry
            first = eight(point, point_l)
            point, point_l = [p + d for p, d in zip(point, stride)], point_l + stride_l
            pair = jnp.concatenate([first, eight(point, point_l)], axis=0)
            point, point_l = [p + d for p, d in zip(point, stride)], point_l + stride_l
            at = pl.ds(pl.multiple_of(16 * block, 16), 16)
            images[i, g, at, :LANES], images[i, g, at, LANES:] = two_parts(pair)
            return point, point_l

        lax.fori_loop(0, width // 16, sixteen, (start, start_l), unroll=8)

    def some_angles(first, carry):
        tables, whole = [], []
        for k in range(bands):
            table = volumes[k][tiles * depth :, :]
            if together < half:
                table = lanes_turned(table, first * (2 * together))
            tables.append(table)
            numbers = table.astype(jnp.int32)
            ahead = pltpu.roll(numbers, Y_MIDDLE - Y_STRIDE, 0)
            here = lax.broadcasted_iota(jnp.int32, (8, LANES), 0)
            whole.append(jnp.where(here == Y_MIDDLE, numbers - (width // 16) * ahead, numbers))

        def value(source, row, i):
            return [[source[g * per + q][row, 2 * ((g * per + q) ^ i) + swap] for q in range(per)] for g in range(groups)]

        scalars = [
            [value(tables, INVERSE, i), value(whole, Y_STRIDE, i), value(whole, Y_MIDDLE, i), value(whole, SHIFT, i)]
            for i in range(together)
        ]
        for i in range(together):
            for g in range(groups):
                gather(i, g, *[entry[g] for entry in scalars[i][:3]])
        for i in range(together):
            j = first * together + i
            total = before[j] if added else None
            for g in range(groups):
                shift_l = by_lane(wide_lane, depth, scalars[i][3][g])
                hits = (place - HALO - shift_l == (wide_lane & (depth - 1))) & keep
                select = jnp.where(hits, 1.0, 0.0).astype(jnp.bfloat16)
                select = jnp.concatenate([select, select], axis=1)
                image = lax.dot_general(select, images[i, g], NT, preferred_element_type=jnp.float32)
                total = image if total is None else total + image
            proj[j] = total
        return carry

    if together == half:
        some_angles(0, 0)
    else:
        lax.fori_loop(0, half // together, some_angles, 0)


def project_back(half, depth, width, swap, entries, held, out, stack, turned, images):
    tiles = width // LANES
    per = LANES // depth
    groups = half // per
    lane = lax.broadcasted_iota(jnp.int32, (8, LANES), 1)
    step = lax.broadcasted_iota(jnp.int32, (8, LANES), 0).astype(jnp.float32)
    place = lax.broadcasted_iota(jnp.int32, (depth, LANES), 0)
    wide_lane = lax.broadcasted_iota(jnp.int32, (depth, LANES), 1)
    select = jnp.where(place == (wide_lane & (depth - 1)), 1.0, 0.0).astype(jnp.bfloat16)
    select = jnp.concatenate([select, select], axis=1)
    turned[:PAD, :] = jnp.zeros((PAD, LANES), jnp.float32)
    turned[PAD + width :, :] = jnp.zeros((PAD, LANES), jnp.float32)
    table = entries[tiles * depth :, :]
    numbers = table.astype(jnp.int32)
    ahead = pltpu.roll(numbers, U_MIDDLE - U_STRIDE, 0)
    here = lax.broadcasted_iota(jnp.int32, (8, LANES), 0)
    numbers = jnp.where(here == U_MIDDLE, numbers - (width // 16) * ahead, numbers)

    def value(source, row, g):
        return [source[row, 2 * (g * per + q) + swap] for q in range(per)]

    total = jnp.zeros((depth, width), jnp.float32)
    for g in range(groups):
        shift = [d + HALO for d in value(numbers, SHIFT, g)]
        stride, start = value(numbers, U_STRIDE, g), value(numbers, U_MIDDLE, g)
        for tile in range(tiles):
            for q in range(per):
                stack[tile, q * depth : (q + 1) * depth, :] = held[g * per + q, tile, pl.ds(shift[q], depth), :]
            turned[PAD + tile * LANES : PAD + (tile + 1) * LANES, :] = stack[tile].T
        inverse_l = by_lane(lane, depth, value(table, INVERSE, g))
        fine = step * by_lane(lane, depth, value(table, MAGNIFICATION, g))
        stride_l = by_lane(lane, depth, stride)
        start_l = by_lane(lane, depth, start)

        def eight(point, point_l):
            base = [jnp.clip((p >> U_BITS) - 1, -PAD, width) + PAD for p in point]
            windows = [turned[pl.ds(base[0] + 8 * r, 8), :] for r in range(3)]
            for q in range(1, per):
                here = lane >= q * depth
                windows = [jnp.where(here, turned[pl.ds(base[q] + 8 * r, 8), :], windows[r]) for r in range(3)]
            target = (point_l & (2**U_BITS - 1)).astype(jnp.float32) * 2.0**-U_BITS + fine
            lower = target.astype(jnp.int32)
            frac = (target - lower.astype(jnp.float32)) * inverse_l
            out = jnp.zeros((8, LANES), jnp.float32)
            for tap in range(4):
                index = lower + tap
                within = index & 7
                value = jnp.where(index < 8, rows_at(windows[0], within), rows_at(windows[1], within))
                if tap >= 2:
                    value = jnp.where(index < 16, value, rows_at(windows[2], within))
                weight = jnp.maximum(0.0, 1.0 - jnp.abs(frac + (1.0 - tap) * inverse_l))
                out += weight * value
            return out

        def sixteen(i, carry):
            point, point_l = carry
            first = eight(point, point_l)
            point, point_l = [p + d for p, d in zip(point, stride)], point_l + stride_l
            pair = jnp.concatenate([first, eight(point, point_l)], axis=0)
            point, point_l = [p + d for p, d in zip(point, stride)], point_l + stride_l
            at = pl.ds(pl.multiple_of(16 * i, 16), 16)
            images[at, :LANES], images[at, LANES:] = two_parts(pair)
            return point, point_l

        lax.fori_loop(0, width // 16, sixteen, (start, start_l), unroll=4)
        total += lax.dot_general(select, images[...], NT, preferred_element_type=jnp.float32)
    out[...] = total * (1.0 / math.sqrt(2 * half))


def residual_kernel(half, depth, width, slabs, *refs):
    info, entries, proj, sums, from_below, from_above = refs[:6]
    others, measured = refs[6 : 6 + slabs - 3], refs[6 + slabs - 3 : 6 + slabs - 3 + half]
    residual, held, other, stack, turned, images, result, sem = refs[6 + slabs - 3 + half :]
    rows = depth + 2 * HALO
    tiles = width // LANES
    edge = (8 + HALO) * half
    column = sums[...] + from_below[edge:, :] + from_above[edge:, :]
    for ref in others:
        column += ref[...]
    keep = info[...] > 0.0
    for j in range(half):
        at = 8 * half + HALO * j
        for tile in range(tiles):
            part = slice(tile * LANES, (tile + 1) * LANES)
            image = jnp.concatenate(
                [
                    proj[j, :8, part] + from_below[8 * j : 8 * j + 8, part],
                    proj[j, 8:depth, part],
                    proj[j, depth:, part] + from_above[8 * j : 8 * j + 8, part],
                ],
                axis=0,
            )
            wanted = jnp.concatenate(
                [from_below[at : at + HALO, part], measured[j][:, part], from_above[at : at + HALO, part]], axis=0
            )
            gain = column[half + j : half + j + 1, part] / column[j : j + 1, part]
            value = jnp.where(keep, (wanted - gain * image) * (1.0 / (2 * half)), 0.0)
            if j == 0:
                result[:, part] = value[HALO : HALO + depth, :]
            held[j, tile] = value
        if j == 0:
            copy = pltpu.make_async_copy(result, residual, sem)
            copy.start()
    project_back(half, depth, width, 1, entries, held, other, stack, turned, images)
    copy.wait()


def own_kernel(half, depth, width, entries, held, out, stack, turned, images):
    project_back(half, depth, width, 0, entries, held, out, stack, turned, images)


def swapped(x, by):
    n = lax.axis_size("xband")
    return lax.ppermute(x, "xband", [(i, i ^ by) for i in range(n)])


def from_slab(x, by):
    n = lax.axis_size("zslab")
    return lax.ppermute(x, "zslab", [(i, (i + by) % n) for i in range(n)])


def shards(volume, measured, magnification, shift_y, shift_z):
    _, depth, width = volume.shape
    n, slabs = lax.axis_size("xband"), lax.axis_size("zslab")
    half = n // 2
    rows = depth + 2 * HALO
    tiles = width // LANES
    f32, bf16 = jnp.float32, jnp.bfloat16
    place = jnp.full((1, 1), lax.axis_index("xband"), jnp.int32)
    info = jnp.where(inside((rows, LANES), depth, lax.axis_index("zslab"), slabs), 1.0, 0.0).astype(f32)

    vmem = pl.BlockSpec(memory_space=pltpu.VMEM)
    params = pltpu.CompilerParams(vmem_limit_bytes=VMEM_LIMIT)

    def on_core(body, shapes, operands, scratch=(), spaces={}, out_spaces={}):
        out = pl.pallas_call(
            body,
            out_shape=[jax.ShapeDtypeStruct(shape, f32) for shape in shapes],
            in_specs=[spaces.get(i, vmem) for i in range(len(operands))],
            out_specs=[out_spaces.get(i, vmem) for i in range(len(shapes))],
            scratch_shapes=scratch,
            compiler_params=params,
        )(*operands)
        return out if len(shapes) > 1 else out[0]

    packed = on_core(
        functools.partial(pack_kernel, depth, width),
        [(tiles * depth + 8, LANES)],
        [
            pltpu.with_memory_space_constraint(x, pltpu.HBM)
            for x in (volume[0], magnification.reshape(1, n), shift_y.reshape(1, n), shift_z.reshape(1, n))
        ]
        + [place],
        [
            pltpu.VMEM((1, n), f32),
            pltpu.VMEM((1, n), jnp.int32),
            pltpu.VMEM((1, n), jnp.int32),
            pltpu.SemaphoreType.DMA((tiles + 3,)),
        ],
        {i: pl.BlockSpec(memory_space=pl.ANY) for i in range(4)},
    )
    far_first = range(half - 1, 0, -1)
    moved = {k: swapped(packed, 2 * k) for k in far_first}
    mine = [packed] + [moved[k] for k in range(1, half)]
    first_swap = swapped(packed, 1)

    view, first_swap = lax.optimization_barrier((measured[0], first_swap))
    moved = {k: swapped(view, 2 * k) for k in far_first}
    views = [view] + [moved[k] for k in range(1, half)]
    theirs = [first_swap] + [swapped(x, 1) for x in mine[1:]]

    def forward(volumes, swap, before):
        bands = len(volumes)
        return on_core(
            functools.partial(forward_kernel, half, depth, width, slabs, bands, swap, len(before)),
            [(half, rows, width)],
            [info] + volumes + before,
            [
                pltpu.VMEM((bands * depth // LANES, width, LANES), f32),
                pltpu.VMEM((min(half, 4), bands * depth // LANES, width, 2 * LANES), bf16),
            ],
        )

    proj = forward(theirs, 1, [forward(mine, 0, [])])
    edge_rows = (8 + HALO + 2) * half
    up, down, sums = on_core(
        functools.partial(edges_kernel, half, depth),
        [(edge_rows, width), (edge_rows, width), (2 * half, width)],
        [proj] + views,
    )
    below, above = from_slab(up, 1), from_slab(down, -1)
    others = [from_slab(sums, k) for k in range(2, slabs - 1)]

    scratch = [
        pltpu.VMEM((tiles, LANES, LANES), f32),
        pltpu.VMEM((width + 2 * PAD, LANES), f32),
        pltpu.VMEM((width, 2 * LANES), bf16),
    ]
    residual, held, other = on_core(
        functools.partial(residual_kernel, half, depth, width, slabs),
        [(depth, width), (half, tiles, rows, LANES), (depth, width)],
        [info, theirs[0], proj, sums, below, above] + others + views,
        scratch + [pltpu.VMEM((depth, width), f32), pltpu.SemaphoreType.DMA],
        out_spaces={0: pl.BlockSpec(memory_space=pl.ANY)},
    )
    from_other = swapped(other, 1)
    own = on_core(
        functools.partial(own_kernel, half, depth, width), [(depth, width)], [mine[0], held], scratch
    )
    return residual[None], (own + from_other)[None]


def solution(mesh):
    return jax.shard_map(
        shards,
        mesh=mesh,
        in_specs=(
            P("xband", "zslab", None),
            P("xband", "zslab", None),
            P(None, "xband"),
            P(None, "xband"),
            P(None, "xband"),
        ),
        out_specs=(P("xband", "zslab", None), P("xband", "zslab", None)),
        check_vma=False,
    )
```

```python
import functools
import math

import jax
import jax.numpy as jnp
from jax import lax
from jax.experimental import pallas as pl
from jax.experimental.pallas import tpu as pltpu
from jax.sharding import PartitionSpec as P

HALO = 4
LANES = 128
SHIFT_MOST = 32
Y_BITS = 21
U_BITS = 20
INVERSE, SHIFT, Y_STRIDE, Y_MIDDLE, U_STRIDE, U_MIDDLE, MAGNIFICATION = range(7)
VMEM_LIMIT = 48 * 1024 * 1024
NT = (((1,), (1,)), ((), ()))


def padding(width):
    return width // 2 + 2 * SHIFT_MOST + 8


def rows_at(tile, index):
    return jnp.take_along_axis(tile, index, axis=0, mode="promise_in_bounds")


def by_lane(lane, depth, values):
    out = jnp.full(lane.shape, values[0])
    for q in range(1, len(values)):
        out = jnp.where(lane >= q * depth, values[q], out)
    return out


def lanes_turned(tile, by):
    lane = lax.broadcasted_iota(jnp.int32, tile.shape, 1)
    return jnp.take_along_axis(tile, lane ^ by, axis=1, mode="promise_in_bounds")


def two_parts(x):
    high = x.astype(jnp.bfloat16)
    return high, (x - high.astype(jnp.float32)).astype(jnp.bfloat16)


def inside(shape, depth, slab, slabs):
    place = lax.broadcasted_iota(jnp.int32, shape, 0)
    return ((place >= HALO) | (slab > 0)) & ((place < HALO + depth) | (slab < slabs - 1))


def pack_kernel(depth, width, volume, *refs):
    small, place, packed, held, sem = refs[:3], refs[3], refs[4], refs[5:8], refs[8]
    magnification, shift_y, shift_z = held
    tiles = width // LANES
    small_copies = [pltpu.make_async_copy(x, y, sem.at[tiles + i]) for i, (x, y) in enumerate(zip(small, held))]
    for copy in small_copies:
        copy.start()
    copies = [
        pltpu.make_async_copy(
            volume.at[:, pl.ds(tile * LANES, LANES)], packed.at[pl.ds(tile * depth, depth)], sem.at[tile]
        )
        for tile in range(tiles)
    ]
    for copy in copies:
        copy.start()
    for copy in small_copies:
        copy.wait()
    mag = magnification[...]
    n = mag.shape[1]
    offset = (width - 1) / 2.0 + shift_y[...].astype(jnp.float32)
    rows = [
        1.0 / mag,
        shift_z[...].astype(jnp.float32),
        jnp.round(8.0 * 2.0**Y_BITS / mag),
        jnp.round((0.5 / mag + offset) * 2.0**Y_BITS),
        jnp.round(8.0 * 2.0**U_BITS * mag),
        jnp.round(((width // 2 - offset) * mag + (width - 1) / 2.0) * 2.0**U_BITS),
        mag,
        mag,
    ]
    table = jnp.concatenate([jnp.concatenate(rows, axis=0), jnp.zeros((8, LANES - n), jnp.float32)], axis=1)
    packed[tiles * depth :, :] = lanes_turned(table, place[...])
    for copy in copies:
        copy.wait()


def edges_kernel(half, depth, *refs):
    proj, measured, (up, down, sums) = refs[0], refs[1 : 1 + half], refs[1 + half :]
    for j in range(half):
        up[8 * j : 8 * j + 8, :] = proj[j, depth : depth + 8, :]
        down[8 * j : 8 * j + 8, :] = proj[j, :8, :]
        at = 8 * half + HALO * j
        up[at : at + HALO, :] = measured[j][depth - HALO :, :]
        down[at : at + HALO, :] = measured[j][:HALO, :]
        sums[j : j + 1, :] = jnp.sum(proj[j], axis=0, keepdims=True)
        sums[half + j : half + j + 1, :] = jnp.sum(measured[j][...], axis=0, keepdims=True)
    at = (8 + HALO) * half
    up[at:, :] = sums[...]
    down[at:, :] = sums[...]


def forward_kernel(half, depth, width, slabs, bands, swap, added, *refs):
    info, volumes = refs[0], refs[1 : 1 + bands]
    before = refs[1 + bands] if added else None
    proj, turned, images = refs[1 + bands + added :]
    tiles = width // LANES
    per = LANES // depth
    groups = bands // per
    rows = depth + 2 * HALO
    for g in range(groups):
        for tile in range(tiles):
            part = slice(tile * depth, (tile + 1) * depth)
            block = jnp.concatenate([volumes[g * per + q][part, :] for q in range(per)], axis=0)
            turned[g, tile * LANES : (tile + 1) * LANES, :] = block.T

    lane = lax.broadcasted_iota(jnp.int32, (8, LANES), 1)
    step = lax.broadcasted_iota(jnp.int32, (8, LANES), 0).astype(jnp.float32)
    place = lax.broadcasted_iota(jnp.int32, (rows, LANES), 0)
    wide_lane = lax.broadcasted_iota(jnp.int32, (rows, LANES), 1)
    keep = info[...] > 0.0
    together = images.shape[0]

    def gather(i, g, inverse, stride, start):
        fine = step * by_lane(lane, depth, inverse)
        stride_l = by_lane(lane, depth, stride)
        start_l = by_lane(lane, depth, start)

        def eight(point, point_l):
            window = turned[g, pl.ds(point[0] >> Y_BITS, 8), :]
            for q in range(1, per):
                window = jnp.where(lane >= q * depth, turned[g, pl.ds(point[q] >> Y_BITS, 8), :], window)
            target = (point_l & (2**Y_BITS - 1)).astype(jnp.float32) * 2.0**-Y_BITS + fine
            lower = target.astype(jnp.int32)
            frac = target - lower.astype(jnp.float32)
            left = rows_at(window, lower)
            return left + frac * (rows_at(window, lower + 1) - left)

        def sixteen(block, carry):
            point, point_l = carry
            first = eight(point, point_l)
            point, point_l = [p + d for p, d in zip(point, stride)], point_l + stride_l
            pair = jnp.concatenate([first, eight(point, point_l)], axis=0)
            point, point_l = [p + d for p, d in zip(point, stride)], point_l + stride_l
            at = pl.ds(pl.multiple_of(16 * block, 16), 16)
            images[i, g, at, :LANES], images[i, g, at, LANES:] = two_parts(pair)
            return point, point_l

        lax.fori_loop(0, width // 16, sixteen, (start, start_l), unroll=8)

    def some_angles(first, carry):
        tables, whole = [], []
        for k in range(bands):
            table = volumes[k][tiles * depth :, :]
            if together < half:
                table = lanes_turned(table, first * (2 * together))
            tables.append(table)
            numbers = table.astype(jnp.int32)
            ahead = pltpu.roll(numbers, Y_MIDDLE - Y_STRIDE, 0)
            here = lax.broadcasted_iota(jnp.int32, (8, LANES), 0)
            whole.append(jnp.where(here == Y_MIDDLE, numbers - (width // 16) * ahead, numbers))

        def value(source, row, i):
            return [[source[g * per + q][row, 2 * ((g * per + q) ^ i) + swap] for q in range(per)] for g in range(groups)]

        scalars = [
            [value(tables, INVERSE, i), value(whole, Y_STRIDE, i), value(whole, Y_MIDDLE, i), value(whole, SHIFT, i)]
            for i in range(together)
        ]
        for i in range(together):
            for g in range(groups):
                gather(i, g, *[entry[g] for entry in scalars[i][:3]])
        for i in range(together):
            j = first * together + i
            total = before[j] if added else None
            for g in range(groups):
                shift_l = by_lane(wide_lane, depth, scalars[i][3][g])
                hits = (place - HALO - shift_l == (wide_lane & (depth - 1))) & keep
                select = jnp.where(hits, 1.0, 0.0).astype(jnp.bfloat16)
                select = jnp.concatenate([select, select], axis=1)
                image = lax.dot_general(select, images[i, g], NT, preferred_element_type=jnp.float32)
                total = image if total is None else total + image
            proj[j] = total
        return carry

    if together == half:
        some_angles(0, 0)
    else:
        lax.fori_loop(0, half // together, some_angles, 0)


def project_back(half, depth, width, swap, entries, held, out, stack, turned, images):
    tiles = width // LANES
    per = LANES // depth
    groups = half // per
    lane = lax.broadcasted_iota(jnp.int32, (8, LANES), 1)
    step = lax.broadcasted_iota(jnp.int32, (8, LANES), 0).astype(jnp.float32)
    place = lax.broadcasted_iota(jnp.int32, (depth, LANES), 0)
    wide_lane = lax.broadcasted_iota(jnp.int32, (depth, LANES), 1)
    select = jnp.where(place == (wide_lane & (depth - 1)), 1.0, 0.0).astype(jnp.bfloat16)
    select = jnp.concatenate([select, select], axis=1)
    pad = padding(width)
    turned[:pad, :] = jnp.zeros((pad, LANES), jnp.float32)
    turned[pad + width :, :] = jnp.zeros((pad, LANES), jnp.float32)
    table = entries[tiles * depth :, :]
    numbers = table.astype(jnp.int32)
    ahead = pltpu.roll(numbers, U_MIDDLE - U_STRIDE, 0)
    here = lax.broadcasted_iota(jnp.int32, (8, LANES), 0)
    numbers = jnp.where(here == U_MIDDLE, numbers - (width // 16) * ahead, numbers)

    def value(source, row, g):
        return [source[row, 2 * (g * per + q) + swap] for q in range(per)]

    total = jnp.zeros((depth, width), jnp.float32)
    for g in range(groups):
        shift = [d + HALO for d in value(numbers, SHIFT, g)]
        stride, start = value(numbers, U_STRIDE, g), value(numbers, U_MIDDLE, g)
        for tile in range(tiles):
            for q in range(per):
                stack[tile, q * depth : (q + 1) * depth, :] = held[g * per + q, tile, pl.ds(shift[q], depth), :]
            turned[pad + tile * LANES : pad + (tile + 1) * LANES, :] = stack[tile].T
        inverse_l = by_lane(lane, depth, value(table, INVERSE, g))
        beside_l, beyond_l = 1.0 - inverse_l, 1.0 - 2.0 * inverse_l
        fine = step * by_lane(lane, depth, value(table, MAGNIFICATION, g))
        stride_l = by_lane(lane, depth, stride)
        start_l = by_lane(lane, depth, start)

        def eight(point, point_l):
            base = [p >> U_BITS for p in point]
            starts = (pad - 1, pad + 7, pad + 1, pad + 9)
            windows = [turned[pl.ds(base[0] + r, 8), :] for r in starts]
            for q in range(1, per):
                here = lane >= q * depth
                windows = [jnp.where(here, turned[pl.ds(base[q] + r, 8), :], w) for r, w in zip(starts, windows)]
            target = (point_l & (2**U_BITS - 1)).astype(jnp.float32) * 2.0**-U_BITS + fine
            lower = target.astype(jnp.int32)
            frac = (target - lower.astype(jnp.float32)) * inverse_l
            weights = [
                jnp.maximum(0.0, beside_l - frac),
                1.0 - frac,
                beside_l + frac,
                jnp.maximum(0.0, beyond_l + frac),
            ]
            out = None
            for tap, weight in enumerate(weights):
                index = lower + tap % 2
                within = index & 7
                pair = windows[tap // 2 * 2 : tap // 2 * 2 + 2]
                value = jnp.where(index < 8, rows_at(pair[0], within), rows_at(pair[1], within))
                out = weight * value if out is None else out + weight * value
            return out

        def sixteen(i, carry):
            point, point_l = carry
            first = eight(point, point_l)
            point, point_l = [p + d for p, d in zip(point, stride)], point_l + stride_l
            pair = jnp.concatenate([first, eight(point, point_l)], axis=0)
            point, point_l = [p + d for p, d in zip(point, stride)], point_l + stride_l
            at = pl.ds(pl.multiple_of(16 * i, 16), 16)
            images[at, :LANES], images[at, LANES:] = two_parts(pair)
            return point, point_l

        lax.fori_loop(0, width // 16, sixteen, (start, start_l), unroll=8)
        total += lax.dot_general(select, images[...], NT, preferred_element_type=jnp.float32)
    out[...] = total * (1.0 / math.sqrt(2 * half))


def residual_kernel(half, depth, width, slabs, *refs):
    info, entries, proj, sums, from_below, from_above = refs[:6]
    others, measured = refs[6 : 6 + slabs - 3], refs[6 + slabs - 3 : 6 + slabs - 3 + half]
    residual, held, other, stack, turned, images, result, sem = refs[6 + slabs - 3 + half :]
    rows = depth + 2 * HALO
    tiles = width // LANES
    edge = (8 + HALO) * half
    column = sums[...] + from_below[edge:, :] + from_above[edge:, :]
    for ref in others:
        column += ref[...]
    keep = info[...] > 0.0
    for j in range(half):
        at = 8 * half + HALO * j
        for tile in range(tiles):
            part = slice(tile * LANES, (tile + 1) * LANES)
            image = jnp.concatenate(
                [
                    proj[j, :8, part] + from_below[8 * j : 8 * j + 8, part],
                    proj[j, 8:depth, part],
                    proj[j, depth:, part] + from_above[8 * j : 8 * j + 8, part],
                ],
                axis=0,
            )
            wanted = jnp.concatenate(
                [from_below[at : at + HALO, part], measured[j][:, part], from_above[at : at + HALO, part]], axis=0
            )
            gain = column[half + j : half + j + 1, part] / column[j : j + 1, part]
            value = jnp.where(keep, (wanted - gain * image) * (1.0 / (2 * half)), 0.0)
            if j == 0:
                result[:, part] = value[HALO : HALO + depth, :]
            held[j, tile] = value
        if j == 0:
            copy = pltpu.make_async_copy(result, residual, sem)
            copy.start()
    project_back(half, depth, width, 1, entries, held, other, stack, turned, images)
    copy.wait()


def own_kernel(half, depth, width, entries, held, out, stack, turned, images):
    project_back(half, depth, width, 0, entries, held, out, stack, turned, images)


def swapped(x, by):
    n = lax.axis_size("xband")
    return lax.ppermute(x, "xband", [(i, i ^ by) for i in range(n)])


def from_slab(x, by):
    n = lax.axis_size("zslab")
    return lax.ppermute(x, "zslab", [(i, (i + by) % n) for i in range(n)])


def shards(volume, measured, magnification, shift_y, shift_z):
    _, depth, width = volume.shape
    n, slabs = lax.axis_size("xband"), lax.axis_size("zslab")
    half = n // 2
    rows = depth + 2 * HALO
    tiles = width // LANES
    f32, bf16 = jnp.float32, jnp.bfloat16
    place = jnp.full((1, 1), lax.axis_index("xband"), jnp.int32)
    info = jnp.where(inside((rows, LANES), depth, lax.axis_index("zslab"), slabs), 1.0, 0.0).astype(f32)

    vmem = pl.BlockSpec(memory_space=pltpu.VMEM)
    params = pltpu.CompilerParams(vmem_limit_bytes=VMEM_LIMIT)

    def on_core(body, shapes, operands, scratch=(), spaces={}, out_spaces={}):
        out = pl.pallas_call(
            body,
            out_shape=[jax.ShapeDtypeStruct(shape, f32) for shape in shapes],
            in_specs=[spaces.get(i, vmem) for i in range(len(operands))],
            out_specs=[out_spaces.get(i, vmem) for i in range(len(shapes))],
            scratch_shapes=scratch,
            compiler_params=params,
        )(*operands)
        return out if len(shapes) > 1 else out[0]

    packed = on_core(
        functools.partial(pack_kernel, depth, width),
        [(tiles * depth + 8, LANES)],
        [
            pltpu.with_memory_space_constraint(x, pltpu.HBM)
            for x in (volume[0], magnification.reshape(1, n), shift_y.reshape(1, n), shift_z.reshape(1, n))
        ]
        + [place],
        [
            pltpu.VMEM((1, n), f32),
            pltpu.VMEM((1, n), jnp.int32),
            pltpu.VMEM((1, n), jnp.int32),
            pltpu.SemaphoreType.DMA((tiles + 3,)),
        ],
        {i: pl.BlockSpec(memory_space=pl.ANY) for i in range(4)},
    )
    far_first = range(half - 1, 0, -1)
    moved = {k: swapped(packed, 2 * k) for k in far_first}
    mine = [packed] + [moved[k] for k in range(1, half)]
    first_swap = swapped(packed, 1)

    view, first_swap = lax.optimization_barrier((measured[0], first_swap))
    moved = {k: swapped(view, 2 * k) for k in far_first}
    views = [view] + [moved[k] for k in range(1, half)]
    theirs = [first_swap] + [swapped(x, 1) for x in mine[1:]]

    def forward(volumes, swap, before):
        bands = len(volumes)
        return on_core(
            functools.partial(forward_kernel, half, depth, width, slabs, bands, swap, len(before)),
            [(half, rows, width)],
            [info] + volumes + before,
            [
                pltpu.VMEM((bands * depth // LANES, width, LANES), f32),
                pltpu.VMEM((min(half, 4), bands * depth // LANES, width, 2 * LANES), bf16),
            ],
        )

    proj = forward(theirs, 1, [forward(mine, 0, [])])
    edge_rows = (8 + HALO + 2) * half
    up, down, sums = on_core(
        functools.partial(edges_kernel, half, depth),
        [(edge_rows, width), (edge_rows, width), (2 * half, width)],
        [proj] + views,
    )
    below, above = from_slab(up, 1), from_slab(down, -1)
    others = [from_slab(sums, k) for k in range(2, slabs - 1)]

    scratch = [
        pltpu.VMEM((tiles, LANES, LANES), f32),
        pltpu.VMEM((width + 2 * padding(width), LANES), f32),
        pltpu.VMEM((width, 2 * LANES), bf16),
    ]
    residual, held, other = on_core(
        functools.partial(residual_kernel, half, depth, width, slabs),
        [(depth, width), (half, tiles, rows, LANES), (depth, width)],
        [info, theirs[0], proj, sums, below, above] + others + views,
        scratch + [pltpu.VMEM((depth, width), f32), pltpu.SemaphoreType.DMA],
        out_spaces={0: pl.BlockSpec(memory_space=pl.ANY)},
    )
    from_other = swapped(other, 1)
    own = on_core(
        functools.partial(own_kernel, half, depth, width), [(depth, width)], [mine[0], held], scratch
    )
    return residual[None], (own + from_other)[None]


def solution(mesh):
    return jax.shard_map(
        shards,
        mesh=mesh,
        in_specs=(
            P("xband", "zslab", None),
            P("xband", "zslab", None),
            P(None, "xband"),
            P(None, "xband"),
            P(None, "xband"),
        ),
        out_specs=(P("xband", "zslab", None), P("xband", "zslab", None)),
        check_vma=False,
    )
```

```python
import functools
import math

import jax
import jax.numpy as jnp
from jax import lax
from jax.experimental import pallas as pl
from jax.experimental.pallas import tpu as pltpu
from jax.sharding import PartitionSpec as P

HALO = 4
LANES = 128
SHIFT_MOST = 32
Y_BITS = 21
U_BITS = 20
INVERSE, SHIFT, Y_STRIDE, Y_MIDDLE, U_STRIDE, U_MIDDLE, MAGNIFICATION = range(7)
VMEM_LIMIT = 48 * 1024 * 1024
NT = (((1,), (1,)), ((), ()))


def padding(width):
    return width // 2 + 2 * SHIFT_MOST + 8


def rows_at(tile, index):
    return jnp.take_along_axis(tile, index, axis=0, mode="promise_in_bounds")


def by_lane(lane, depth, values):
    out = jnp.full(lane.shape, values[0])
    for q in range(1, len(values)):
        out = jnp.where(lane >= q * depth, values[q], out)
    return out


def lanes_turned(tile, by):
    lane = lax.broadcasted_iota(jnp.int32, tile.shape, 1)
    return jnp.take_along_axis(tile, lane ^ by, axis=1, mode="promise_in_bounds")


def two_parts(x):
    high = x.astype(jnp.bfloat16)
    return high, (x - high.astype(jnp.float32)).astype(jnp.bfloat16)


def inside(shape, depth, slab, slabs):
    place = lax.broadcasted_iota(jnp.int32, shape, 0)
    return ((place >= HALO) | (slab > 0)) & ((place < HALO + depth) | (slab < slabs - 1))


def pack_kernel(depth, width, volume, *refs):
    small, place, packed, held, sem = refs[:3], refs[3], refs[4], refs[5:8], refs[8]
    magnification, shift_y, shift_z = held
    tiles = width // LANES
    small_copies = [pltpu.make_async_copy(x, y, sem.at[tiles + i]) for i, (x, y) in enumerate(zip(small, held))]
    for copy in small_copies:
        copy.start()
    copies = [
        pltpu.make_async_copy(
            volume.at[:, pl.ds(tile * LANES, LANES)], packed.at[pl.ds(tile * depth, depth)], sem.at[tile]
        )
        for tile in range(tiles)
    ]
    for copy in copies:
        copy.start()
    for copy in small_copies:
        copy.wait()
    mag = magnification[...]
    n = mag.shape[1]
    offset = (width - 1) / 2.0 + shift_y[...].astype(jnp.float32)
    rows = [
        1.0 / mag,
        shift_z[...].astype(jnp.float32),
        jnp.round(8.0 * 2.0**Y_BITS / mag),
        jnp.round((0.5 / mag + offset) * 2.0**Y_BITS),
        jnp.round(8.0 * 2.0**U_BITS * mag),
        jnp.round(((width // 2 - offset) * mag + (width - 1) / 2.0) * 2.0**U_BITS),
        mag,
        mag,
    ]
    table = jnp.concatenate([jnp.concatenate(rows, axis=0), jnp.zeros((8, LANES - n), jnp.float32)], axis=1)
    packed[tiles * depth :, :] = lanes_turned(table, place[...])
    for copy in copies:
        copy.wait()


def image_edges_kernel(half, depth, info, proj, first, second, sums):
    width = proj.shape[2]
    odd = jnp.broadcast_to(info[:1, :1] >= 2.0, (8, width))
    for j in range(half):
        up, down = proj[j, depth : depth + 8, :], proj[j, :8, :]
        first[8 * j : 8 * j + 8, :] = jnp.where(odd, down, up)
        second[8 * j : 8 * j + 8, :] = jnp.where(odd, up, down)
        sums[j : j + 1, :] = jnp.sum(proj[j], axis=0, keepdims=True)
    first[8 * half :, :] = sums[...]
    second[8 * half :, :] = sums[...]


def measured_edges_kernel(half, depth, info, image_sums, *refs):
    measured, (first, second, sums) = refs[:half], refs[half:]
    width = sums.shape[1]
    odd = jnp.broadcast_to(info[:1, :1] >= 2.0, (HALO, width))
    sums[:half, :] = image_sums[...]
    for j in range(half):
        up, down = measured[j][depth - HALO :, :], measured[j][:HALO, :]
        first[HALO * j : HALO * j + HALO, :] = jnp.where(odd, down, up)
        second[HALO * j : HALO * j + HALO, :] = jnp.where(odd, up, down)
        sums[half + j : half + j + 1, :] = jnp.sum(measured[j][...], axis=0, keepdims=True)
    first[HALO * half :, :] = sums[half:, :]
    second[HALO * half :, :] = sums[half:, :]


def forward_kernel(half, depth, width, slabs, bands, swap, added, *refs):
    info, volumes = refs[0], refs[1 : 1 + bands]
    before = refs[1 + bands] if added else None
    proj, turned, images = refs[1 + bands + added :]
    tiles = width // LANES
    per = LANES // depth
    groups = bands // per
    rows = depth + 2 * HALO
    for g in range(groups):
        for tile in range(tiles):
            part = slice(tile * depth, (tile + 1) * depth)
            block = jnp.concatenate([volumes[g * per + q][part, :] for q in range(per)], axis=0)
            turned[g, tile * LANES : (tile + 1) * LANES, :] = block.T

    lane = lax.broadcasted_iota(jnp.int32, (8, LANES), 1)
    step = lax.broadcasted_iota(jnp.int32, (8, LANES), 0).astype(jnp.float32)
    place = lax.broadcasted_iota(jnp.int32, (rows, LANES), 0)
    wide_lane = lax.broadcasted_iota(jnp.int32, (rows, LANES), 1)
    keep = (info[...] == 1.0) | (info[...] == 3.0)
    together = images.shape[0]

    def gather(i, g, inverse, stride, start):
        fine = step * by_lane(lane, depth, inverse)
        stride_l = by_lane(lane, depth, stride)
        start_l = by_lane(lane, depth, start)

        def eight(point, point_l):
            window = turned[g, pl.ds(point[0] >> Y_BITS, 8), :]
            for q in range(1, per):
                window = jnp.where(lane >= q * depth, turned[g, pl.ds(point[q] >> Y_BITS, 8), :], window)
            target = (point_l & (2**Y_BITS - 1)).astype(jnp.float32) * 2.0**-Y_BITS + fine
            lower = target.astype(jnp.int32)
            frac = target - lower.astype(jnp.float32)
            left = rows_at(window, lower)
            return left + frac * (rows_at(window, lower + 1) - left)

        def sixteen(block, carry):
            point, point_l = carry
            first = eight(point, point_l)
            point, point_l = [p + d for p, d in zip(point, stride)], point_l + stride_l
            pair = jnp.concatenate([first, eight(point, point_l)], axis=0)
            point, point_l = [p + d for p, d in zip(point, stride)], point_l + stride_l
            at = pl.ds(pl.multiple_of(16 * block, 16), 16)
            images[i, g, at, :LANES], images[i, g, at, LANES:] = two_parts(pair)
            return point, point_l

        lax.fori_loop(0, width // 16, sixteen, (start, start_l), unroll=True)

    def some_angles(first, carry):
        tables, whole = [], []
        for k in range(bands):
            table = volumes[k][tiles * depth :, :]
            if together < half:
                table = lanes_turned(table, first * (2 * together))
            tables.append(table)
            numbers = table.astype(jnp.int32)
            ahead = pltpu.roll(numbers, Y_MIDDLE - Y_STRIDE, 0)
            here = lax.broadcasted_iota(jnp.int32, (8, LANES), 0)
            whole.append(jnp.where(here == Y_MIDDLE, numbers - (width // 16) * ahead, numbers))

        def value(source, row, i):
            return [[source[g * per + q][row, 2 * ((g * per + q) ^ i) + swap] for q in range(per)] for g in range(groups)]

        scalars = [
            [value(tables, INVERSE, i), value(whole, Y_STRIDE, i), value(whole, Y_MIDDLE, i), value(whole, SHIFT, i)]
            for i in range(together)
        ]
        for i in range(together):
            for g in range(groups):
                gather(i, g, *[entry[g] for entry in scalars[i][:3]])
        for i in range(together):
            j = first * together + i
            total = before[j] if added else None
            for g in range(groups):
                shift_l = by_lane(wide_lane, depth, scalars[i][3][g])
                hits = (place - HALO - shift_l == (wide_lane & (depth - 1))) & keep
                select = jnp.where(hits, 1.0, 0.0).astype(jnp.bfloat16)
                select = jnp.concatenate([select, select], axis=1)
                image = lax.dot_general(select, images[i, g], NT, preferred_element_type=jnp.float32)
                total = image if total is None else total + image
            proj[j] = total
        return carry

    if together == half:
        some_angles(0, 0)
    else:
        lax.fori_loop(0, half // together, some_angles, 0)


def project_back(half, depth, width, swap, unroll, entries, held, out, stack, turned, images):
    tiles = width // LANES
    per = LANES // depth
    groups = half // per
    lane = lax.broadcasted_iota(jnp.int32, (8, LANES), 1)
    step = lax.broadcasted_iota(jnp.int32, (8, LANES), 0).astype(jnp.float32)
    place = lax.broadcasted_iota(jnp.int32, (depth, LANES), 0)
    wide_lane = lax.broadcasted_iota(jnp.int32, (depth, LANES), 1)
    select = jnp.where(place == (wide_lane & (depth - 1)), 1.0, 0.0).astype(jnp.bfloat16)
    select = jnp.concatenate([select, select], axis=1)
    pad = padding(width)
    turned[:pad, :] = jnp.zeros((pad, LANES), jnp.float32)
    turned[pad + width :, :] = jnp.zeros((pad, LANES), jnp.float32)
    table = entries[tiles * depth :, :]
    numbers = table.astype(jnp.int32)
    ahead = pltpu.roll(numbers, U_MIDDLE - U_STRIDE, 0)
    here = lax.broadcasted_iota(jnp.int32, (8, LANES), 0)
    numbers = jnp.where(here == U_MIDDLE, numbers - (width // 16) * ahead, numbers)

    def value(source, row, g):
        return [source[row, 2 * (g * per + q) + swap] for q in range(per)]

    total = jnp.zeros((depth, width), jnp.float32)
    for g in range(groups):
        shift = [d + HALO for d in value(numbers, SHIFT, g)]
        stride, start = value(numbers, U_STRIDE, g), value(numbers, U_MIDDLE, g)
        for tile in range(tiles):
            for q in range(per):
                stack[tile, q * depth : (q + 1) * depth, :] = held[g * per + q, tile, pl.ds(shift[q], depth), :]
            turned[pad + tile * LANES : pad + (tile + 1) * LANES, :] = stack[tile].T
        inverse_l = by_lane(lane, depth, value(table, INVERSE, g))
        beside_l, beyond_l = 1.0 - inverse_l, 1.0 - 2.0 * inverse_l
        fine = step * by_lane(lane, depth, value(table, MAGNIFICATION, g))
        stride_l = by_lane(lane, depth, stride)
        start_l = by_lane(lane, depth, start)

        def eight(point, point_l):
            base = [p >> U_BITS for p in point]
            starts = (pad - 1, pad + 7, pad + 1, pad + 9)
            windows = [turned[pl.ds(base[0] + r, 8), :] for r in starts]
            for q in range(1, per):
                here = lane >= q * depth
                windows = [jnp.where(here, turned[pl.ds(base[q] + r, 8), :], w) for r, w in zip(starts, windows)]
            target = (point_l & (2**U_BITS - 1)).astype(jnp.float32) * 2.0**-U_BITS + fine
            lower = target.astype(jnp.int32)
            frac = (target - lower.astype(jnp.float32)) * inverse_l
            weights = [
                jnp.maximum(0.0, beside_l - frac),
                1.0 - frac,
                beside_l + frac,
                jnp.maximum(0.0, beyond_l + frac),
            ]
            out = None
            for tap, weight in enumerate(weights):
                index = lower + tap % 2
                within = index & 7
                pair = windows[tap // 2 * 2 : tap // 2 * 2 + 2]
                value = jnp.where(index < 8, rows_at(pair[0], within), rows_at(pair[1], within))
                out = weight * value if out is None else out + weight * value
            return out

        def sixteen(i, carry):
            point, point_l = carry
            first = eight(point, point_l)
            point, point_l = [p + d for p, d in zip(point, stride)], point_l + stride_l
            pair = jnp.concatenate([first, eight(point, point_l)], axis=0)
            point, point_l = [p + d for p, d in zip(point, stride)], point_l + stride_l
            at = pl.ds(pl.multiple_of(16 * i, 16), 16)
            images[at, :LANES], images[at, LANES:] = two_parts(pair)
            return point, point_l

        lax.fori_loop(0, width // 16, sixteen, (start, start_l), unroll=unroll)
        total += lax.dot_general(select, images[...], NT, preferred_element_type=jnp.float32)
    out[...] = total * (1.0 / math.sqrt(2 * half))


def residual_kernel(half, depth, width, slabs, *refs):
    info, entries, proj, sums, first, second, first_m, second_m = refs[:8]
    refs = refs[2:]
    others, measured = refs[6 : 6 + slabs - 3], refs[6 + slabs - 3 : 6 + slabs - 3 + half]
    residual, held, other, stack, turned, images, result, sem = refs[6 + slabs - 3 + half :]
    rows = depth + 2 * HALO
    tiles = width // LANES
    image_sum = sums[:half, :] + first[8 * half :, :] + second[8 * half :, :]
    measured_sum = sums[half:, :] + first_m[HALO * half :, :] + second_m[HALO * half :, :]
    odd = jnp.broadcast_to(info[:1, :1] >= 2.0, (8, LANES))
    for ref in others:
        image_sum += ref[:half, :]
        measured_sum += ref[half:, :]
    keep = (info[...] == 1.0) | (info[...] == 3.0)
    for j in range(half):
        at = HALO * j
        for tile in range(tiles):
            part = slice(tile * LANES, (tile + 1) * LANES)
            one, two = first[8 * j : 8 * j + 8, part], second[8 * j : 8 * j + 8, part]
            below, above = jnp.where(odd, one, two), jnp.where(odd, two, one)
            image = jnp.concatenate(
                [proj[j, :8, part] + below, proj[j, 8:depth, part], proj[j, depth:, part] + above], axis=0
            )
            one, two = first_m[at : at + HALO, part], second_m[at : at + HALO, part]
            below, above = jnp.where(odd[:HALO], one, two), jnp.where(odd[:HALO], two, one)
            wanted = jnp.concatenate([below, measured[j][:, part], above], axis=0)
            gain = measured_sum[j : j + 1, part] / image_sum[j : j + 1, part]
            value = jnp.where(keep, (wanted - gain * image) * (1.0 / (2 * half)), 0.0)
            if j == 0:
                result[:, part] = value[HALO : HALO + depth, :]
            held[j, tile] = value
        if j == 0:
            copy = pltpu.make_async_copy(result, residual, sem)
            copy.start()
    project_back(half, depth, width, 1, 8, entries, held, other, stack, turned, images)
    copy.wait()


def own_kernel(half, depth, width, entries, held, out, stack, turned, images):
    project_back(half, depth, width, 0, width // 16, entries, held, out, stack, turned, images)


def swapped(x, by):
    n = lax.axis_size("xband")
    return lax.ppermute(x, "xband", [(i, i ^ by) for i in range(n)])


def from_slab(x, by):
    n = lax.axis_size("zslab")
    return lax.ppermute(x, "zslab", [(i, (i + by) % n) for i in range(n)])


def between(x, odd):
    n = lax.axis_size("zslab")
    return lax.ppermute(x, "zslab", [(i, (i + (1 if i % 2 == odd else -1)) % n) for i in range(n)])


def shards(volume, measured, magnification, shift_y, shift_z):
    _, depth, width = volume.shape
    n, slabs = lax.axis_size("xband"), lax.axis_size("zslab")
    half = n // 2
    rows = depth + 2 * HALO
    tiles = width // LANES
    f32, bf16 = jnp.float32, jnp.bfloat16
    place = jnp.full((1, 1), lax.axis_index("xband"), jnp.int32)
    slab = lax.axis_index("zslab")
    info = jnp.where(inside((rows, LANES), depth, slab, slabs), 1.0, 0.0).astype(f32) + 2.0 * ((slab + 1) % 2).astype(f32)

    vmem = pl.BlockSpec(memory_space=pltpu.VMEM)
    params = pltpu.CompilerParams(vmem_limit_bytes=VMEM_LIMIT)

    def on_core(body, shapes, operands, scratch=(), spaces={}, out_spaces={}):
        out = pl.pallas_call(
            body,
            out_shape=[jax.ShapeDtypeStruct(shape, f32) for shape in shapes],
            in_specs=[spaces.get(i, vmem) for i in range(len(operands))],
            out_specs=[out_spaces.get(i, vmem) for i in range(len(shapes))],
            scratch_shapes=scratch,
            compiler_params=params,
        )(*operands)
        return out if len(shapes) > 1 else out[0]

    packed = on_core(
        functools.partial(pack_kernel, depth, width),
        [(tiles * depth + 8, LANES)],
        [
            pltpu.with_memory_space_constraint(x, pltpu.HBM)
            for x in (volume[0], magnification.reshape(1, n), shift_y.reshape(1, n), shift_z.reshape(1, n))
        ]
        + [place],
        [
            pltpu.VMEM((1, n), f32),
            pltpu.VMEM((1, n), jnp.int32),
            pltpu.VMEM((1, n), jnp.int32),
            pltpu.SemaphoreType.DMA((tiles + 3,)),
        ],
        {i: pl.BlockSpec(memory_space=pl.ANY) for i in range(4)},
    )
    far_first = range(half - 1, 0, -1)
    moved = {k: swapped(packed, 2 * k) for k in far_first}
    mine = [packed] + [moved[k] for k in range(1, half)]
    first_swap = swapped(packed, 1)

    view, first_swap = lax.optimization_barrier((measured[0], first_swap))
    moved = {k: swapped(view, 2 * k) for k in far_first}
    views = [view] + [moved[k] for k in range(1, half)]
    theirs = [first_swap] + [swapped(x, 1) for x in mine[1:]]

    def forward(volumes, swap, before):
        bands = len(volumes)
        return on_core(
            functools.partial(forward_kernel, half, depth, width, slabs, bands, swap, len(before)),
            [(half, rows, width)],
            [info] + volumes + before,
            [
                pltpu.VMEM((bands * depth // LANES, width, LANES), f32),
                pltpu.VMEM((min(half, 4), bands * depth // LANES, width, 2 * LANES), bf16),
            ],
        )

    proj = forward(theirs, 1, [forward(mine, 0, [])])
    first, second, image_sums = on_core(
        functools.partial(image_edges_kernel, half, depth), [(9 * half, width)] * 2 + [(half, width)], [info, proj]
    )
    first, second = between(first, 1), between(second, 0)
    first_m, second_m, sums = on_core(
        functools.partial(measured_edges_kernel, half, depth),
        [((HALO + 1) * half, width)] * 2 + [(2 * half, width)],
        [info, image_sums] + views,
    )
    first_m, second_m = between(first_m, 1), between(second_m, 0)
    others = [from_slab(sums, k) for k in range(2, slabs - 1)]

    scratch = [
        pltpu.VMEM((tiles, LANES, LANES), f32),
        pltpu.VMEM((width + 2 * padding(width), LANES), f32),
        pltpu.VMEM((width, 2 * LANES), bf16),
    ]
    residual, held, other = on_core(
        functools.partial(residual_kernel, half, depth, width, slabs),
        [(depth, width), (half, tiles, rows, LANES), (depth, width)],
        [info, theirs[0], proj, sums, first, second, first_m, second_m] + others + views,
        scratch + [pltpu.VMEM((depth, width), f32), pltpu.SemaphoreType.DMA],
        out_spaces={0: pl.BlockSpec(memory_space=pl.ANY)},
    )
    from_other = swapped(other, 1)
    own = on_core(
        functools.partial(own_kernel, half, depth, width), [(depth, width)], [mine[0], held], scratch
    )
    return residual[None], (own + from_other)[None]


def solution(mesh):
    return jax.shard_map(
        shards,
        mesh=mesh,
        in_specs=(
            P("xband", "zslab", None),
            P("xband", "zslab", None),
            P(None, "xband"),
            P(None, "xband"),
            P(None, "xband"),
        ),
        out_specs=(P("xband", "zslab", None), P("xband", "zslab", None)),
        check_vma=False,
    )
```
